256 devices in a mesh: tm: 64 (over x, z, core), region: 4 (over y).
Axes of the slice: x: 4, y: 4, z: 8, core: 2. Of those that a mesh axis runs over, the one named last changes fastest.
Arguments:
- solution: float32 [8192, 4096], P('tm', 'region'), may hold values from -6 to 6
- residual: float32 [8192, 4096], P('tm', 'region'), may hold values from -50 to 50
- direction: float32 [8192, 4096], P('tm', 'region'), may hold values from -50 to 50
- decay: float32 [8192, 4096], P('tm', 'region'), may hold values from 0 to 1, as said below
- spatial: bfloat16 [4096, 4096], P('region'), may hold values from -1 to 2, as said below
- tiles: bfloat16 [64, 4, 8, 128, 512], P('tm', 'region'), may hold values from -0.1875 to 0.1875
- tile_block: int32 [64, 4, 8], P('tm', 'region'), may hold values from 0 to 7
- tile_time: int32 [64, 4, 8], P('tm', 'region'), may hold values from 0 to 383
- tile_cell: int32 [64, 4, 8], P('tm', 'region'), may hold values from 0 to 1
- tile_count: int32 [64, 4], P('tm', 'region'), may hold values from 1 to 8, as said below
- noise_inv: float32 [512, 128], P('tm'), may hold values from 0.25 to 2
Outputs:
- solution_new: float32 [8192, 4096], P('tm', 'region')
- residual_new: float32 [8192, 4096], P('tm', 'region')
- direction_new: float32 [8192, 4096], P('tm', 'region')
The draws below stay inside these ranges and needn't reach their ends.
Inputs may be any that keep to these rules, and one draw needn't show every extreme that they name: Slots 0 to tile_count - 1 of a window and region hold tiles, the rest are padding; some window and region has 8. `decay`: strictly between 0 and 1. `spatial`: symmetric.
All inputs are finite; a program needn't handle non-finite values.
Results may differ from the reference program's by a relative error of at most 0.0028.
Values may be sent and summed in bfloat16 or wider, within the bound.
A program may use at most 64 MiB of HBM per device.

```python
import math
import jax
import jax.numpy as jnp
from jax import lax

FB = 512
SB = 128
RC = 1024
TW = 128
NSB = 8
TCAP = 8
BACK = 2
WINDOWS = 64
REGIONS = 4
EMISSION_EPOCHS = 8192
CELLS = 4096
SPAN = 384
CBLK = 2


def scaled_field(key):
    key_a, key_b = jax.random.split(key)
    ramp_up = jnp.arange(EMISSION_EPOCHS, dtype=jnp.float32) / max(EMISSION_EPOCHS - 1, 1)
    row_scale = 10.0 ** ramp_up
    entries = jnp.clip(jax.random.normal(key_a, (EMISSION_EPOCHS, CELLS), jnp.float32), -5.0, 5.0)
    col_scale = 10.0 ** jax.random.uniform(key_b, (CELLS,), jnp.float32)
    return entries * row_scale[:, None] * col_scale[None, :] / 10.0


def draw_residual(key, part):
    return scaled_field(jax.random.fold_in(key, 11))


def draw_direction(key, part):
    return scaled_field(jax.random.fold_in(key, 23))


def draw_decay(key, part):
    key_a, key_b, key_c, key_d, sampler_seed_number5, key_f = jax.random.split(key, 6)
    slow_share = 0.5
    is_slow = jax.random.uniform(key_a, (CELLS,), jnp.float32) < slow_share
    slow_rate = jnp.exp(jax.random.uniform(key_b, (CELLS,), jnp.float32, math.log(0.1), math.log(0.8))) / EMISSION_EPOCHS
    fast_rate = jnp.exp(jax.random.uniform(key_c, (CELLS,), jnp.float32, math.log(1.0 / 40.0), math.log(0.2)))
    base_rate = jnp.where(is_slow, slow_rate, fast_rate)
    jitter = jax.random.uniform(key_d, (EMISSION_EPOCHS, CELLS), jnp.float32, 0.5, 1.5)
    decay_val = jnp.exp(-base_rate[None, :] * jitter)
    pulse_onset_index = jax.random.randint(sampler_seed_number5, (2,), 0, EMISSION_EPOCHS)
    cut_indices = jax.random.uniform(key_f, (2, CELLS), jnp.float32, 0.6, 0.8)
    epoch_index = jnp.arange(EMISSION_EPOCHS)[:, None]
    front_cut_index = jnp.where(epoch_index == pulse_onset_index[0], cut_indices[0][None, :], 1.0)
    rear_cut_index = jnp.where(epoch_index == pulse_onset_index[1], cut_indices[1][None, :], 1.0)
    return decay_val * front_cut_index * rear_cut_index


def draw_spatial(key, part):
    key_a, key_b = jax.random.split(key)
    entries = jnp.clip(jax.random.normal(key_a, (CELLS, CELLS), jnp.float32), -5.0, 5.0)
    symmetric = (entries + entries.T) / math.sqrt(2.0)
    diag_gain = jax.random.uniform(key_b, (CELLS,), jnp.float32, 1.0, 1.5)
    return (jnp.eye(CELLS, dtype=jnp.float32) * diag_gain[None, :] + 0.5 * symmetric / math.sqrt(CELLS)).astype(jnp.bfloat16)


def draw_tile_count(key, part):
    key_a, key_b = jax.random.split(key)
    counts = jax.random.randint(key_a, (WINDOWS, REGIONS), TCAP // 8, TCAP * 5 // 8 + 1)
    chosen_dev = jax.random.randint(key_b, (), 0, WINDOWS * REGIONS)
    flat_ids = jnp.arange(WINDOWS * REGIONS).reshape(WINDOWS, REGIONS)
    return jnp.where(flat_ids == chosen_dev, TCAP, counts).astype(jnp.int32)


def place_ends(values, rng, smallest, largest):
    longest = values.shape.index(max(values.shape))
    spots = []
    for shift in (0, 1):
        where = [jax.random.randint(jax.random.fold_in(rng, axis), (), 0, length) for axis, length in enumerate(values.shape)]
        where[longest] = (where[longest] + shift) % values.shape[longest]
        spots.append(tuple(where))
    return values.at[spots[0]].set(smallest).at[spots[1]].set(largest)


def steps_of(own_key, extent, cuts, smallest, high):
    loudness = 1.0
    for position, parts in cuts:
        draws = jax.random.uniform(jax.random.fold_in(jax.random.fold_in(own_key, 6), position), (parts,), jnp.float32, smallest / len(cuts), high / len(cuts))
        loudness = loudness * jnp.repeat(jnp.exp(draws), extent[position] // parts).reshape((-1,) + (1,) * (len(extent) - 1 - position))
    return loudness


def bell_draw(stream_key, extent, scale, limit, shards=(), held_as=jnp.bfloat16):
    gain = steps_of(stream_key, extent, shards, -0.22, 0.18) if shards else 1.0
    result = jax.random.normal(stream_key, extent, jnp.float32) * scale * gain
    return jnp.minimum(jnp.maximum(result, -limit), limit).astype(held_as)


def setup_inputs(seed: int = 0) -> dict:
    arg_keys = jax.random.split(jax.random.key(seed), 12)
    solution = bell_draw(arg_keys[0], (EMISSION_EPOCHS, CELLS), 1.0, 6.0, ((0, 64), (1, 4)), jnp.float32)
    residual = draw_residual(jax.random.fold_in(arg_keys[11], 71), 0)
    direction = draw_direction(jax.random.fold_in(arg_keys[11], 71), 0)
    decay = draw_decay(jax.random.fold_in(arg_keys[11], 71), 0)
    spatial = draw_spatial(jax.random.fold_in(arg_keys[11], 71), 0)
    tiles = bell_draw(arg_keys[5], (WINDOWS, REGIONS, TCAP, SB, FB), (2 * FB) ** -0.5, 0.1875, ((0, 64), (1, 4)))
    tile_block = place_ends(jax.random.randint(arg_keys[6], (WINDOWS, REGIONS, TCAP), 0, NSB), jax.random.fold_in(arg_keys[6], 1), 0, NSB - 1).astype(jnp.int32)
    tile_time = place_ends(jax.random.randint(arg_keys[7], (WINDOWS, REGIONS, TCAP), 0, SPAN), jax.random.fold_in(arg_keys[7], 1), 0, SPAN - 1).astype(jnp.int32)
    tile_cell = place_ends(jax.random.randint(arg_keys[8], (WINDOWS, REGIONS, TCAP), 0, CBLK), jax.random.fold_in(arg_keys[8], 1), 0, CBLK - 1).astype(jnp.int32)
    tile_count = draw_tile_count(jax.random.fold_in(arg_keys[11], 71), 0)
    noise_inv = jnp.clip(jnp.exp(math.log(2.0) - 2.0794415 * jax.random.uniform(arg_keys[10], (WINDOWS * NSB, SB), jnp.float32) ** steps_of(arg_keys[10], (WINDOWS * NSB, SB), ((0, 64),), -0.2, 0.2)), 0.25, 2.0)
    return dict(solution=solution, residual=residual, direction=direction, decay=decay, spatial=spatial, tiles=tiles, tile_block=tile_block, tile_time=tile_time, tile_cell=tile_cell, tile_count=tile_count, noise_inv=noise_inv)


def reference(solution, residual, direction, decay, spatial, tiles, tile_block, tile_time, tile_cell, tile_count, noise_inv):
    precise = lax.Precision.HIGHEST
    gain_in = jnp.sqrt(1.0 - decay * decay)
    spatial_wide = spatial.astype(jnp.float32)
    dir_half = direction.astype(jnp.bfloat16)
    mixed_cells = jnp.dot(dir_half.astype(jnp.float32), spatial_wide.T, precision=precise, preferred_element_type=jnp.float32)

    def forward_step(state, inputs):
        state = inputs[0] * state + inputs[1]
        return (state, state)
    zero_row = jnp.zeros((CELLS,), jnp.float32)
    _, filtered = lax.scan(forward_step, zero_row, (decay, gain_in * mixed_cells))
    coarse = filtered.astype(jnp.bfloat16)
    padded = jnp.concatenate([jnp.zeros((BACK * TW, CELLS), jnp.bfloat16), coarse], axis=0)
    span_len = (BACK + 1) * TW
    cell_blocks = RC // FB
    slot_ids = jnp.arange(TCAP, dtype=jnp.int32)
    block_ids = jnp.arange(NSB, dtype=jnp.int32)
    place_ids = jnp.arange(span_len * cell_blocks, dtype=jnp.int32)

    def window_obs(window_idx):
        window = lax.dynamic_slice_in_dim(padded, (window_idx * TW).astype(jnp.int32), span_len, 0)
        running = jnp.zeros((NSB, SB), jnp.float32)
        for region in range(REGIONS):
            cells_of = window[:, region * RC:(region + 1) * RC].reshape(span_len, cell_blocks, FB)
            is_live = slot_ids < tile_count[window_idx, region]
            chosen = cells_of[tile_time[window_idx, region], tile_cell[window_idx, region]].astype(jnp.float32)
            partial_value = jnp.einsum('jkc,jc->jk', tiles[window_idx, region].astype(jnp.float32), chosen, precision=precise)
            onehot = ((tile_block[window_idx, region][None, :] == block_ids[:, None]) & is_live[None, :]).astype(jnp.float32)
            running = running + jnp.dot(onehot, partial_value, precision=precise)
        return running
    observed = lax.map(window_obs, jnp.arange(WINDOWS, dtype=jnp.int32))
    weighted = (observed.reshape(WINDOWS * NSB, SB) * noise_inv).astype(jnp.bfloat16).reshape(WINDOWS, NSB, SB)

    def window_back(accum, window_idx):
        columns = []
        for region in range(REGIONS):
            is_live = slot_ids < tile_count[window_idx, region]
            picked = weighted[window_idx][tile_block[window_idx, region]].astype(jnp.float32)
            partial_value = jnp.einsum('jkc,jk->jc', tiles[window_idx, region].astype(jnp.float32), picked, precision=precise)
            epoch_index = tile_time[window_idx, region] * cell_blocks + tile_cell[window_idx, region]
            onehot = ((epoch_index[None, :] == place_ids[:, None]) & is_live[None, :]).astype(jnp.float32)
            columns.append(jnp.dot(onehot, partial_value, precision=precise).reshape(span_len, RC))
        block_sum = jnp.concatenate(columns, axis=1)
        first_row = (window_idx * TW).astype(jnp.int32)
        current = lax.dynamic_slice_in_dim(accum, first_row, span_len, 0)
        accum = lax.dynamic_update_slice_in_dim(accum, current + block_sum, first_row, 0)
        return (accum, None)
    accum, _ = lax.scan(window_back, jnp.zeros((EMISSION_EPOCHS + BACK * TW, CELLS), jnp.float32), jnp.arange(WINDOWS, dtype=jnp.int32))
    adjoint = accum[BACK * TW:]

    def backward_step(carry, inputs):
        held_sum = inputs[1] + carry
        return (inputs[0] * held_sum, held_sum)
    _, held_sum = lax.scan(backward_step, zero_row, (decay, adjoint), reverse=True)
    pulled = (gain_in * held_sum).astype(jnp.bfloat16)
    spread = jnp.dot(pulled.astype(jnp.float32), spatial_wide, precision=precise, preferred_element_type=jnp.float32)
    op_image = direction + spread
    norm_old = jnp.sum(residual * residual)
    curvature = jnp.sum(direction * op_image)
    step_len = norm_old / curvature
    solution_new = solution + step_len * direction
    residual_new = residual - step_len * op_image
    norm_new = jnp.sum(residual_new * residual_new)
    direction_new = residual_new + norm_new / norm_old * direction
    return (solution_new, residual_new, direction_new)
```

```python
import jax
import jax.numpy as jnp
from jax import lax
from jax.experimental import pallas as pl
from jax.experimental.pallas import tpu as pltpu
from jax.sharding import PartitionSpec as P

MESH = pl.DeviceIdType.MESH
TW = 128
RC = 1024
FB = 512
SLOTS = 8
LINE = 16
LINES = 4
REGIONS = 4
WINDOWS = LINE * LINES
CH = 8
ST = TW // CH
PIECES = RC // 128
DEAD = -8192
F32 = jnp.float32
BF16 = jnp.bfloat16
NT = (((1,), (1,)), ((), ()))
TN = (((0,), (0,)), ((), ()))


def kernel(
    dir_h, res_h, dec_h, spa_h, tiles_h, tblock, ttime, tcell, tcount, noise,
    img, ab,
    dirv, resv, decv, spa, tiles, xa, xb, dp, gp, fp, rp, mx, hx, fstep, bstep, ends,
    abuf, gabuf, bbuf, tbuf, cbuf, ubuf, tabs, chs, bks, obs, red1, red2, sel,
    lsem, gas, gar, gbs, gbr, as_, ar, a2s, a2r, bs, br, b2s, b2r, cs, cr, c2s, c2r,
    ts, tr, hs, hr, ks, kr, os_, or_, r1s, r1r, r2s, r2r,
):
    tm = lax.axis_index("tm")
    r = lax.axis_index("region")
    gx = tm // LINE
    gi = lax.rem(tm, LINE)

    loads = [pltpu.make_async_copy(dir_h, dirv, lsem.at[0])]
    for k in range(REGIONS):
        src = lax.rem(r + REGIONS - k, REGIONS)
        cols = pl.ds(pl.multiple_of(src * RC, RC), RC)
        loads.append(pltpu.make_async_copy(spa_h.at[:, cols], spa.at[k], lsem.at[1 + k]))
    loads.append(pltpu.make_async_copy(tiles_h.at[0, 0], tiles, lsem.at[5]))
    loads.append(pltpu.make_async_copy(res_h, resv, lsem.at[6]))
    for n in range(PIECES):
        loads.append(pltpu.make_async_copy(dec_h.at[:, 128 * n : 128 * (n + 1)], decv.at[n], lsem.at[7 + n]))
    load_dir, load_spa, load_tiles, load_res, load_dec = loads[0], loads[1:5], loads[5], loads[6], loads[7:]
    for c in loads:
        c.start()

    line_peers = [(gx * LINE + lax.rem(gi + k, LINE), r) for k in range(1, LINE)]
    cross_peers = [(lax.rem(gx + k, LINES) * LINE + gi, r) for k in range(1, LINES)]
    region_peers = [(tm, lax.rem(r + k, REGIONS)) for k in range(1, REGIONS)]
    plane_peers = [
        (lax.rem(gx + kx, LINES) * LINE + gi, lax.rem(r + ky, REGIONS))
        for kx in range(LINES)
        for ky in range(REGIONS)
        if kx or ky
    ]
    later = [(lax.rem(tm + d, WINDOWS), r) for d in (1, 2)]
    sooner = [(lax.rem(tm + WINDOWS - d, WINDOWS), r) for d in (1, 2)]

    barrier = pltpu.get_barrier_semaphore()
    everyone = line_peers + plane_peers + later + sooner
    for peer in everyone:
        pl.semaphore_signal(barrier, inc=1, device_id=peer, device_id_type=MESH)

    def send(src, dst, ss, rs, peer):
        c = pltpu.make_async_remote_copy(
            src_ref=src, dst_ref=dst, send_sem=ss, recv_sem=rs, device_id=peer, device_id_type=MESH
        )
        c.start()
        return c

    def to_all(ref, ss, rs, peers):
        return [send(ref, ref, ss.at[k], rs.at[k], peer) for k, peer in enumerate(peers)]

    def wait_all(copies):
        for c in copies:
            c.wait()

    sub8 = lax.broadcasted_iota(jnp.int32, (CH, RC), 0)
    sub = lax.broadcasted_iota(jnp.int32, (8, 128), 0)

    load_dir.wait()
    row = lax.broadcasted_iota(jnp.int32, (TW, TW), 0)
    col = lax.broadcasted_iota(jnp.int32, (TW, TW), 1)
    moved = jnp.where(lax.rem(row, CH) * ST + row // CH == col, 1.0, 0.0).astype(BF16)
    xa[0] = jnp.dot(moved, dirv[...].astype(BF16), preferred_element_type=F32).astype(BF16)

    pl.semaphore_wait(barrier, len(everyone))

    low, high = pl.ds(0, TW // 2), pl.ds(TW // 2, TW // 2)
    right = (tm, lax.rem(r + 1, REGIONS))
    left = (tm, lax.rem(r + REGIONS - 1, REGIONS))

    def gather_start(x, ss, rs):
        return [
            send(x.at[0, low], x.at[1, low], ss.at[0], rs.at[0], right),
            send(x.at[0, high], x.at[3, high], ss.at[1], rs.at[1], left),
            send(x.at[0, high], x.at[1, high], ss.at[2], rs.at[2], right),
            send(x.at[0, low], x.at[3, low], ss.at[3], rs.at[3], left),
        ]

    def gather_pass(x, ss, rs, copies):
        copies[0].wait_recv()
        copies.append(send(x.at[1, low], x.at[2, low], ss.at[4], rs.at[4], right))
        copies[1].wait_recv()
        copies.append(send(x.at[3, high], x.at[2, high], ss.at[5], rs.at[5], left))

    def multiply(x, k, first):
        def tile(n, _):
            cols = pl.ds(pl.multiple_of(n * 256, 256), 256)
            part = lax.dot_general(x[k], spa[k, cols, :], NT, preferred_element_type=F32)
            if first:
                mx[:, cols] = part
            else:
                mx[:, cols] += part
            return 0

        lax.fori_loop(0, RC // 256, tile, 0)

    def gather_multiply(x, ss, rs, copies, between):
        between()
        gather_pass(x, ss, rs, copies)
        multiply(x, 0, True)
        copies[2].wait_recv()
        multiply(x, 1, False)
        copies[3].wait_recv()
        multiply(x, 3, False)
        copies[4].wait_recv()
        copies[5].wait_recv()
        multiply(x, 2, False)
        for c in copies:
            c.wait_send()

    def steps(i):
        return slice(CH * i, CH * (i + 1))

    def prepare():
        table = jnp.full((8, 128), DEAD, jnp.int32)
        for s in range(SLOTS):
            key = jnp.where(s < tcount[0, 0], ttime[0, 0, s] * 2 + tcell[0, 0, s], DEAD)
            table = jnp.where(sub == s, key, table)
        tabs[0] = table
        table_copies = [
            send(tabs.at[0], tabs.at[d], ts.at[d - 1], tr.at[d - 1], sooner[d - 1]) for d in (1, 2)
        ]
        for load in load_dec:
            load.wait()
        f = jnp.ones((CH, RC), F32)
        for i in range(ST):
            d = jnp.concatenate([decv[n, pl.ds(i, CH, stride=ST), :] for n in range(PIECES)], axis=1)
            dp[steps(i), :] = d
            gp[steps(i), :] = jnp.sqrt(1.0 - d * d)
            f = f * d
            fp[steps(i), :] = f
        total = f
        for n, k in enumerate((1, 2, 4)):
            fstep[n] = f
            f = f * jnp.where(sub8 >= k, pltpu.roll(f, k, 0), 1.0)
        ends[0] = jnp.where(sub8 >= 1, pltpu.roll(f, 1, 0), 1.0)
        abuf[gi] = f[CH - 1 : CH, :]
        factor_copies = to_all(abuf.at[gi], as_, ar, line_peers)
        b = total
        for n, k in enumerate((1, 2, 4)):
            bstep[n] = b
            b = b * jnp.where(sub8 < CH - k, pltpu.roll(b, CH - k, 0), 1.0)
        ends[1] = jnp.where(sub8 < CH - 1, pltpu.roll(b, CH - 1, 0), 1.0)
        rest = jnp.ones((CH, RC), F32)
        for i in reversed(range(ST)):
            rp[steps(i), :] = rest
            rest = rest * dp[steps(i), :]
        wait_all(factor_copies)
        before = jnp.ones((1, RC), F32)
        after = jnp.ones((1, RC), F32)
        for j in range(LINE):
            before = before * jnp.where(j < gi, abuf[j], 1.0)
            after = after * jnp.where(j > gi, abuf[j], 1.0)
        ends[2, 0:1, :] = before
        ends[3, 0:1, :] = after
        gabuf[gx] = before * after * abuf[gi]
        cross_copies = to_all(gabuf.at[gx], a2s, a2r, cross_peers)
        wait_all(table_copies)
        time_of = lax.broadcasted_iota(jnp.int32, (8, 128), 1)
        time_of = lax.rem(time_of, CH) * ST + time_of // CH
        for d in (1, 2):
            tabs[d] = jnp.where(tm + d < WINDOWS, tabs[d], DEAD)
        for d in range(3):
            local = lax.shift_right_arithmetic(tabs[d], 1) + (d - 2) * TW
            sel[8 * d : 8 * d + 8, :] = jnp.where(local == time_of, 1.0, 0.0)
        sel[24:32, :] = jnp.zeros((8, 128), F32)
        wait_all(cross_copies)

    def second_block(d):
        cell = lax.bitwise_and(tabs[d], 1) == 1
        return jnp.concatenate([cell] * (FB // 128), axis=1)

    copies = gather_start(xa, gas, gar)
    for c in load_spa:
        c.wait()
    gather_multiply(xa, gas, gar, copies, prepare)

    o = jnp.zeros((CH, RC), F32)
    for i in range(ST):
        o = dp[steps(i), :] * o + gp[steps(i), :] * mx[steps(i), :]
        mx[steps(i), :] = o
    for n, k in enumerate((1, 2, 4)):
        o = o + fstep[n] * jnp.where(sub8 >= k, pltpu.roll(o, k, 0), 0.0)
    bbuf[gi] = o[CH - 1 : CH, :]
    line_copies = to_all(bbuf.at[gi], bs, br, line_peers)
    entry = jnp.where(sub8 >= 1, pltpu.roll(o, 1, 0), 0.0)
    wait_all(line_copies)
    run = jnp.zeros((1, RC), F32)
    mine = run
    for j in range(LINE):
        mine = jnp.where(j == gi, run, mine)
        run = abuf[j] * run + bbuf[j]
    tbuf[gx] = run
    cross_copies = to_all(tbuf.at[gx], b2s, b2r, cross_peers)
    wait_all(cross_copies)
    run = jnp.zeros((1, RC), F32)
    for j in range(LINES):
        run = jnp.where(j < gx, gabuf[j] * run + tbuf[j], run)
    entry = entry + ends[0] * (mine + ends[2, 0:1, :] * run)
    for i in range(ST):
        mx[steps(i), :] = mx[steps(i), :] + fp[steps(i), :] * entry
    coarse = mx[...].astype(BF16)

    chosen = jnp.dot(sel[...].astype(BF16), coarse, preferred_element_type=F32)
    for d in range(3):
        rows = chosen[8 * d : 8 * d + 8, :]
        part = jnp.where(second_block(d), rows[:, FB:], rows[:, :FB])
        chs[3 + d if d else 0] = part
    row_copies = [send(chs.at[3 + d], chs.at[d], hs.at[d - 1], hr.at[d - 1], later[d - 1]) for d in (1, 2)]
    load_tiles.wait()
    wait_all(row_copies)
    picked = chs[0] + chs[1] + chs[2]

    sub_fb = lax.broadcasted_iota(jnp.int32, (8, FB), 0)
    seen = jnp.zeros((8, 128), F32)
    for s in range(SLOTS):
        lhs = jnp.where(sub_fb == tblock[0, 0, s], picked[s : s + 1, :], 0.0).astype(BF16)
        seen = seen + lax.dot_general(lhs, tiles[s], NT, preferred_element_type=F32)
    obs[r] = seen
    wait_all(to_all(obs.at[r], os_, or_, region_peers))
    observed = ((obs[0] + obs[1]) + obs[2]) + obs[3]
    weighted = (observed * noise[...]).astype(BF16).astype(F32)

    back = jnp.zeros((8, FB), F32)
    for s in range(SLOTS):
        row = jnp.sum(jnp.where(sub == tblock[0, 0, s], weighted, 0.0), axis=0, keepdims=True)
        lhs = jnp.where((sub == s) & (s < tcount[0, 0]), row, 0.0).astype(BF16)
        back = back + jnp.dot(lhs, tiles[s], preferred_element_type=F32)
    bks[0] = back
    wait_all([send(bks.at[0], bks.at[d], ks.at[d - 1], kr.at[d - 1], sooner[d - 1]) for d in (1, 2)])
    rows = []
    for d in range(3):
        second = second_block(d)
        rows.append(
            jnp.concatenate([jnp.where(second, 0.0, bks[d]), jnp.where(second, bks[d], 0.0)], axis=1)
        )
    rows.append(jnp.zeros((8, RC), F32))
    rows = jnp.concatenate(rows, axis=0)
    hot = sel[...].astype(BF16)
    first = rows.astype(BF16)
    left_over = rows - first.astype(F32)
    second = left_over.astype(BF16)
    third = (left_over - second.astype(F32)).astype(BF16)
    hx[...] = (
        lax.dot_general(hot, third, TN, preferred_element_type=F32)
        + lax.dot_general(hot, second, TN, preferred_element_type=F32)
    ) + lax.dot_general(hot, first, TN, preferred_element_type=F32)

    c = jnp.zeros((CH, RC), F32)
    for i in reversed(range(ST)):
        h = hx[steps(i), :] + c
        hx[steps(i), :] = h
        c = dp[steps(i), :] * h
    for n, k in enumerate((1, 2, 4)):
        c = c + bstep[n] * jnp.where(sub8 < CH - k, pltpu.roll(c, CH - k, 0), 0.0)
    cbuf[gi] = c[0:1, :]
    line_copies = to_all(cbuf.at[gi], cs, cr, line_peers)
    entry = jnp.where(sub8 < CH - 1, pltpu.roll(c, CH - 1, 0), 0.0)
    wait_all(line_copies)
    run = jnp.zeros((1, RC), F32)
    mine = run
    for j in reversed(range(LINE)):
        mine = jnp.where(j == gi, run, mine)
        run = abuf[j] * run + cbuf[j]
    ubuf[gx] = run
    wait_all(to_all(ubuf.at[gx], c2s, c2r, cross_peers))
    run = jnp.zeros((1, RC), F32)
    for j in reversed(range(LINES)):
        run = jnp.where(j > gx, gabuf[j] * run + ubuf[j], run)
    entry = entry + ends[1] * (mine + ends[3, 0:1, :] * run)
    for i in range(ST):
        held = hx[steps(i), :] + rp[steps(i), :] * entry
        hx[steps(i), :] = gp[steps(i), :] * held
    xb[0] = lax.dot_general(moved, hx[...].astype(BF16), TN, preferred_element_type=F32).astype(BF16)

    copies = gather_start(xb, gbs, gbr)

    def norms():
        load_res.wait()

    gather_multiply(xb, gbs, gbr, copies, norms)
    image = dirv[...] + mx[...]
    img[...] = image

    def whole(x):
        return jnp.sum(jnp.sum(x, axis=0, keepdims=True), axis=1, keepdims=True)

    def inverse(x):
        ok = x > 1e-37
        return jnp.where(ok, 1.0 / jnp.where(ok, x, 1.0), 0.0)

    res = resv[...]
    largest = jnp.max(jnp.max(jnp.abs(image), axis=0, keepdims=True), axis=1, keepdims=True)
    scaled = image * inverse(largest)
    stats = jnp.where(sub == 0, whole(res * res), 0.0)
    stats = jnp.where(sub == 1, whole(dirv[...] * image), stats)
    stats = jnp.where(sub == 2, whole(res * image), stats)
    stats = jnp.where(sub == 3, whole(scaled * scaled), stats)
    stats = jnp.where(sub == 4, largest, stats)

    def merged(buf, count):
        top = buf[0, 4:5, :]
        for j in range(1, count):
            top = jnp.maximum(top, buf[j, 4:5, :])
        inv = inverse(top)
        out = jnp.zeros((8, 128), F32)
        for j in range(count):
            scale = buf[j, 4:5, :] * inv
            out = out + jnp.where(sub == 3, buf[j] * (scale * scale), buf[j])
        return jnp.where(sub == 4, top, out)

    red1[gi] = stats
    wait_all(to_all(red1.at[gi], r1s, r1r, line_peers))
    here = gx * REGIONS + r
    red2[here] = merged(red1, LINE)
    wait_all(to_all(red2.at[here], r2s, r2r, plane_peers))
    stats = merged(red2, LINES * REGIONS)
    norm_old = stats[0:1, :]
    alpha = norm_old / stats[1:2, :]
    reach = alpha * stats[4:5, :]
    norm_new = jnp.maximum((norm_old - 2.0 * (alpha * stats[2:3, :])) + reach * (reach * stats[3:4, :]), 0.0)
    ab[...] = jnp.where(sub == 0, alpha, norm_new / norm_old)


def body(
    solution, residual, direction, decay, spatial, tiles,
    tile_block, tile_time, tile_cell, tile_count, noise_inv,
):
    any_spec = pl.BlockSpec(memory_space=pl.ANY)
    smem = pl.BlockSpec(memory_space=pltpu.SMEM)
    vmem = pl.BlockSpec(memory_space=pltpu.VMEM)
    vector = (1, RC)
    dma = pltpu.SemaphoreType.DMA
    sems = [7 + PIECES, 6, 6, 6, 6]
    for n in (LINE - 1, LINES - 1) * 3 + (2, 2, 2, REGIONS - 1, LINE - 1, LINES * REGIONS - 1):
        sems += [n, n]
    image, ab = pl.pallas_call(
        kernel,
        out_shape=(
            jax.ShapeDtypeStruct((TW, RC), F32),
            jax.ShapeDtypeStruct((8, 128), F32),
        ),
        in_specs=[any_spec] * 5 + [smem] * 4 + [vmem],
        out_specs=(vmem, vmem),
        scratch_shapes=[
            pltpu.VMEM((TW, RC), F32),
            pltpu.VMEM((TW, RC), F32),
            pltpu.VMEM((PIECES, TW, 128), F32),
            pltpu.VMEM((REGIONS, RC, RC), BF16),
            pltpu.VMEM((SLOTS, 128, FB), BF16),
            pltpu.VMEM((REGIONS, TW, RC), BF16),
            pltpu.VMEM((REGIONS, TW, RC), BF16),
            pltpu.VMEM((TW, RC), F32),
            pltpu.VMEM((TW, RC), F32),
            pltpu.VMEM((TW, RC), F32),
            pltpu.VMEM((TW, RC), F32),
            pltpu.VMEM((TW, RC), F32),
            pltpu.VMEM((TW, RC), F32),
            pltpu.VMEM((3, CH, RC), F32),
            pltpu.VMEM((3, CH, RC), F32),
            pltpu.VMEM((4, CH, RC), F32),
            pltpu.VMEM((LINE,) + vector, F32),
            pltpu.VMEM((LINES,) + vector, F32),
            pltpu.VMEM((LINE,) + vector, F32),
            pltpu.VMEM((LINES,) + vector, F32),
            pltpu.VMEM((LINE,) + vector, F32),
            pltpu.VMEM((LINES,) + vector, F32),
            pltpu.VMEM((3, 8, 128), jnp.int32),
            pltpu.VMEM((6, 8, FB), F32),
            pltpu.VMEM((3, 8, FB), F32),
            pltpu.VMEM((REGIONS, 8, 128), F32),
            pltpu.VMEM((LINE, 8, 128), F32),
            pltpu.VMEM((LINES * REGIONS, 8, 128), F32),
            pltpu.VMEM((32, 128), F32),
        ]
        + [dma((n,)) for n in sems],
        compiler_params=pltpu.CompilerParams(
            collective_id=0, has_side_effects=True, vmem_limit_bytes=48 << 20
        ),
        cost_estimate=pl.CostEstimate(
            flops=4 * TW * RC * RC * REGIONS, bytes_accessed=12 << 20, transcendentals=TW * RC
        ),
        name="cg_step",
    )(direction, residual, decay, spatial, tiles, tile_block, tile_time, tile_cell, tile_count, noise_inv)
    alpha = ab[0, 0]
    beta = ab[1, 0]
    residual_new = residual - alpha * image
    return (solution + alpha * direction, residual_new, residual_new + beta * direction)


def solution(mesh):
    return jax.shard_map(
        body,
        mesh=mesh,
        in_specs=(
            P("tm", "region"),
            P("tm", "region"),
            P("tm", "region"),
            P("tm", "region"),
            P("region", None),
            P("tm", "region", None, None, None),
            P("tm", "region", None),
            P("tm", "region", None),
            P("tm", "region", None),
            P("tm", "region"),
            P("tm", None),
        ),
        out_specs=(P("tm", "region"), P("tm", "region"), P("tm", "region")),
        check_vma=False,
    )
```

```python
import jax
import jax.numpy as jnp
from jax import lax
from jax.experimental import pallas as pl
from jax.experimental.pallas import tpu as pltpu
from jax.sharding import PartitionSpec as P

MESH = pl.DeviceIdType.MESH
TW = 128
RC = 1024
FB = 512
SLOTS = 8
LINE = 16
LINES = 4
REGIONS = 4
WINDOWS = LINE * LINES
CH = 8
ST = TW // CH
PIECES = RC // 128
DEAD = -8192
F32 = jnp.float32
BF16 = jnp.bfloat16
NT = (((1,), (1,)), ((), ()))
TN = (((0,), (0,)), ((), ()))


def kernel(
    dir_h, res_h, dec_h, spa_h, tiles_h, tblock_h, ttime_h, tcell_h, tcount_h, noise_h,
    img, alpha_o, beta_o,
    tblock, ttime, tcell, tcount, noise,
    imgv, dirv, resv, decv, spa, tiles, xa, xb, dp, gp, fp, rp, mx, hx, fstep, bstep, ends,
    abuf, gabuf, bbuf, tbuf, cbuf, ubuf, tabs, chs, ffs, bks, near, obs, red1, red2, sel,
    lsem, gas, gar, gbs, gbr, as_, ar, a2s, a2r, bs, br, b2s, b2r, cs, cr, c2s, c2r,
    ts, tr, hs, hr, fs, fr, ks, kr, ns, nr, os_, or_, r1s, r1r, r2s, r2r,
):
    tm = lax.axis_index("tm")
    r = lax.axis_index("region")
    gx = tm // LINE
    gi = lax.rem(tm, LINE)

    loads = [pltpu.make_async_copy(dir_h, dirv, lsem.at[0])]
    for k in range(REGIONS):
        src = lax.rem(r + REGIONS - k, REGIONS)
        cols = pl.ds(pl.multiple_of(src * RC, RC), RC)
        loads.append(pltpu.make_async_copy(spa_h.at[:, cols], spa.at[k], lsem.at[1 + k]))
    loads.append(pltpu.make_async_copy(tiles_h.at[0, 0], tiles, lsem.at[5]))
    loads.append(pltpu.make_async_copy(res_h, resv, lsem.at[6]))
    for n in range(PIECES):
        loads.append(pltpu.make_async_copy(dec_h.at[:, 128 * n : 128 * (n + 1)], decv.at[n], lsem.at[7 + n]))
    small = ((tcount_h, tcount), (ttime_h, ttime), (tcell_h, tcell), (tblock_h, tblock), (noise_h, noise))
    for n, (there, here) in enumerate(small):
        loads.append(pltpu.make_async_copy(there, here, lsem.at[7 + PIECES + n]))
    load_small = loads[7 + PIECES :]
    load_dir, load_spa, load_tiles, load_res, load_dec = loads[0], loads[1:5], loads[5], loads[6], loads[7 : 7 + PIECES]
    for c in loads:
        c.start()

    line_peers = [(gx * LINE + lax.rem(gi + k, LINE), r) for k in range(1, LINE)]
    cross_peers = [(lax.rem(gx + k, LINES) * LINE + gi, r) for k in range(1, LINES)]
    region_peers = [(tm, lax.rem(r + k, REGIONS)) for k in range(1, REGIONS)]
    plane_peers = [
        (lax.rem(gx + kx, LINES) * LINE + gi, lax.rem(r + ky, REGIONS))
        for kx in range(LINES)
        for ky in range(REGIONS)
        if kx or ky
    ]
    later = [(lax.rem(tm + d, WINDOWS), r) for d in (1, 2)]
    sooner = [(lax.rem(tm + WINDOWS - d, WINDOWS), r) for d in (1, 2)]

    barrier = pltpu.get_barrier_semaphore()
    everyone = line_peers + plane_peers + later + sooner
    for peer in everyone:
        pl.semaphore_signal(barrier, inc=1, device_id=peer, device_id_type=MESH)

    sent = []

    def send(src, dst, ss, rs, peer):
        c = pltpu.make_async_remote_copy(
            src_ref=src, dst_ref=dst, send_sem=ss, recv_sem=rs, device_id=peer, device_id_type=MESH
        )
        c.start()
        sent.append(c)
        return c

    def to_all(ref, ss, rs, peers):
        return [send(ref, ref, ss.at[k], rs.at[k], peer) for k, peer in enumerate(peers)]

    def received(copies):
        for c in copies:
            c.wait_recv()

    sub8 = lax.broadcasted_iota(jnp.int32, (CH, RC), 0)
    sub = lax.broadcasted_iota(jnp.int32, (8, 128), 0)

    load_dir.wait()
    row = lax.broadcasted_iota(jnp.int32, (TW, TW), 0)
    col = lax.broadcasted_iota(jnp.int32, (TW, TW), 1)
    moved = jnp.where(lax.rem(row, CH) * ST + row // CH == col, 1.0, 0.0).astype(BF16)
    xa[0] = jnp.dot(moved, dirv[...].astype(BF16), preferred_element_type=F32).astype(BF16)

    pl.semaphore_wait(barrier, len(everyone))

    low, high = pl.ds(0, TW // 2), pl.ds(TW // 2, TW // 2)
    right = (tm, lax.rem(r + 1, REGIONS))
    left = (tm, lax.rem(r + REGIONS - 1, REGIONS))

    def gather_start(x, ss, rs):
        return [
            send(x.at[0, low], x.at[1, low], ss.at[0], rs.at[0], right),
            send(x.at[0, high], x.at[3, high], ss.at[1], rs.at[1], left),
            send(x.at[0, high], x.at[1, high], ss.at[2], rs.at[2], right),
            send(x.at[0, low], x.at[3, low], ss.at[3], rs.at[3], left),
        ]

    def gather_pass(x, ss, rs, copies):
        copies[0].wait_recv()
        copies.append(send(x.at[1, low], x.at[2, low], ss.at[4], rs.at[4], right))
        copies[1].wait_recv()
        copies.append(send(x.at[3, high], x.at[2, high], ss.at[5], rs.at[5], left))

    def multiply(x, k, first):
        def tile(n, _):
            cols = pl.ds(pl.multiple_of(n * 256, 256), 256)
            part = lax.dot_general(x[k], spa[k, cols, :], NT, preferred_element_type=F32)
            if first:
                mx[:, cols] = part
            else:
                mx[:, cols] += part
            return 0

        lax.fori_loop(0, RC // 256, tile, 0)

    def steps(i):
        return slice(CH * i, CH * (i + 1))

    def thirds(x):
        first = x.astype(BF16)
        left_over = x - first.astype(F32)
        second = left_over.astype(BF16)
        return first, second, (left_over - second.astype(F32)).astype(BF16)

    def second_block(d):
        cell = lax.bitwise_and(tabs[d], 1) == 1
        return jnp.concatenate([cell] * (FB // 128), axis=1)

    def hand_on(dense, buf, ss, rs):
        first, second, third = thirds(dense)
        hot = sel[...].astype(BF16)
        rows = (
            jnp.dot(hot, third, preferred_element_type=F32) + jnp.dot(hot, second, preferred_element_type=F32)
        ) + jnp.dot(hot, first, preferred_element_type=F32)
        for d in range(3):
            part = rows[8 * d : 8 * d + 8, :]
            buf[2 + d if d else 0] = jnp.where(second_block(d), part[:, FB:], part[:, :FB])
        return [send(buf.at[2 + d], buf.at[d], ss.at[d - 1], rs.at[d - 1], later[d - 1]) for d in (1, 2)]

    copies = gather_start(xa, gas, gar)

    for load in load_small:
        load.wait()
    table = jnp.full((8, 128), DEAD, jnp.int32)
    for s in range(SLOTS):
        key = jnp.where(s < tcount[0, 0], ttime[0, 0, s] * 2 + tcell[0, 0, s], DEAD)
        table = jnp.where(sub == s, key, table)
    tabs[0] = table
    table_copies = [
        send(tabs.at[0], tabs.at[d], ts.at[d - 1], tr.at[d - 1], sooner[d - 1]) for d in (1, 2)
    ]
    for load in load_dec:
        load.wait()
    f = jnp.ones((CH, RC), F32)
    for i in range(ST):
        d = jnp.concatenate([decv[n, pl.ds(i, CH, stride=ST), :] for n in range(PIECES)], axis=1)
        dp[steps(i), :] = d
        f = f * d
        fp[steps(i), :] = f
    total = f
    for n, k in enumerate((1, 2, 4)):
        fstep[n] = f
        f = f * jnp.where(sub8 >= k, pltpu.roll(f, k, 0), 1.0)
    abuf[gi] = f[CH - 1 : CH, :]
    factor_copies = to_all(abuf.at[gi], as_, ar, line_peers)
    chunk_before = jnp.where(sub8 >= 1, pltpu.roll(f, 1, 0), 1.0)
    for i in range(ST):
        hx[steps(i), :] = fp[steps(i), :] * chunk_before
    b = total
    for n, k in enumerate((1, 2, 4)):
        bstep[n] = b
        b = b * jnp.where(sub8 < CH - k, pltpu.roll(b, CH - k, 0), 1.0)
    ends[1] = jnp.where(sub8 < CH - 1, pltpu.roll(b, CH - 1, 0), 1.0)

    received(table_copies)
    time_of = lax.broadcasted_iota(jnp.int32, (8, 128), 1)
    time_of = lax.rem(time_of, CH) * ST + time_of // CH
    for d in (1, 2):
        tabs[d] = jnp.where(tm + d < WINDOWS, tabs[d], DEAD)
    for d in range(3):
        local = lax.shift_right_arithmetic(tabs[d], 1) + (d - 2) * TW
        sel[8 * d : 8 * d + 8, :] = jnp.where(local == time_of, 1.0, 0.0)
    sel[24:32, :] = jnp.zeros((8, 128), F32)
    factor_rows = hand_on(hx[...], ffs, fs, fr)
    gather_pass(xa, gas, gar, copies)
    for load in load_spa:
        load.wait()

    multiply(xa, 0, True)
    received(factor_copies)
    run = jnp.ones((1, RC), F32)
    places = [run] * 3
    for j in range(LINE):
        for n in range(3):
            places[n] = jnp.where(j == gi - n, run, places[n])
        if j >= LINE - 2:
            gabuf[gx, LINE - j] = run
        run = run * abuf[j]
    gabuf[gx, 0] = run
    gabuf[gx, 3] = abuf[LINE - 1]
    gabuf[gx, 4] = abuf[LINE - 2]
    cross_copies = to_all(gabuf.at[gx], a2s, a2r, cross_peers)
    for n in range(3):
        ends[2, n : n + 1, :] = places[n]
    run = jnp.ones((1, RC), F32)
    for j in range(3, LINE):
        run = run * jnp.where(j >= gi + 3, abuf[j - 2], 1.0)
    ends[3, 0:1, :] = run
    rest = jnp.ones((CH, RC), F32)
    for i in reversed(range(ST)):
        d = dp[steps(i), :]
        gp[steps(i), :] = jnp.sqrt(1.0 - d * d)
        rp[steps(i), :] = rest
        rest = rest * d
    received(copies[2:3])
    multiply(xa, 1, False)
    received(copies[3:4])
    multiply(xa, 3, False)
    received(copies[4:6])
    multiply(xa, 2, False)

    o = jnp.zeros((CH, RC), F32)
    for i in range(ST):
        o = dp[steps(i), :] * o + gp[steps(i), :] * mx[steps(i), :]
        mx[steps(i), :] = o
    for n, k in enumerate((1, 2, 4)):
        o = o + fstep[n] * jnp.where(sub8 >= k, pltpu.roll(o, k, 0), 0.0)
    bbuf[gi] = o[CH - 1 : CH, :]
    line_copies = to_all(bbuf.at[gi], bs, br, line_peers)

    entry = jnp.where(sub8 >= 1, pltpu.roll(o, 1, 0), 0.0)
    for i in range(ST):
        mx[steps(i), :] = mx[steps(i), :] + fp[steps(i), :] * entry
    row_copies = hand_on(mx[...], chs, hs, hr)
    received(cross_copies)
    received(factor_rows)
    before = lax.rem(gx + LINES - 1, LINES)
    ends[3, 1:2, :] = jnp.where(gi >= 1, abuf[lax.rem(gi + LINE - 1, LINE)], gabuf[before, 3])
    ends[3, 2:3, :] = jnp.where(
        gi >= 2, abuf[lax.rem(gi + LINE - 2, LINE)], jnp.where(gi == 1, gabuf[before, 3], gabuf[before, 4])
    )
    received(line_copies)
    run = jnp.zeros((1, RC), F32)
    places = [run] * 3
    for j in range(LINE):
        for n in range(3):
            places[n] = jnp.where(j == gi - n, run, places[n])
        if j >= LINE - 2:
            tbuf[gx, LINE - j] = run
        run = abuf[j] * run + bbuf[j]
    tbuf[gx, 0] = run
    cross_copies = to_all(tbuf.at[gx], b2s, b2r, cross_peers)
    received(row_copies)
    received(cross_copies)
    run = jnp.zeros((1, RC), F32)
    line_before = run
    for j in range(LINES):
        line_before = jnp.where(j == gx - 1, run, line_before)
        run = jnp.where(j < gx, gabuf[j, 0] * run + tbuf[j, 0], run)
    last, last_but = [tbuf[before, n] + gabuf[before, n] * line_before for n in (1, 2)]
    inside = [places[n] + ends[2, n : n + 1, :] * run for n in range(3)]
    entering = [
        inside[0],
        jnp.where(gi >= 1, inside[1], last),
        jnp.where(gi >= 2, inside[2], jnp.where(gi == 1, last, last_but)),
    ]
    own_second = second_block(0)
    picked = jnp.zeros((8, FB), F32)
    for d in range(3):
        state = jnp.where(own_second, entering[d][:, FB:], entering[d][:, :FB])
        picked = picked + (chs[d] + ffs[d] * state)
    load_tiles.wait()

    sub_fb = lax.broadcasted_iota(jnp.int32, (8, FB), 0)
    seen = jnp.zeros((8, 128), F32)
    for s in range(SLOTS):
        lhs = jnp.where(sub_fb == tblock[0, 0, s], picked[s : s + 1, :], 0.0).astype(BF16)
        seen = seen + lax.dot_general(lhs, tiles[s], NT, preferred_element_type=F32)
    obs[r] = seen
    received(to_all(obs.at[r], os_, or_, region_peers))
    observed = ((obs[0] + obs[1]) + obs[2]) + obs[3]
    weighted = (observed * noise[...]).astype(BF16).astype(F32)

    back = jnp.zeros((8, FB), F32)
    for s in range(SLOTS):
        row = jnp.sum(jnp.where(sub == tblock[0, 0, s], weighted, 0.0), axis=0, keepdims=True)
        lhs = jnp.where((sub == s) & (s < tcount[0, 0]), row, 0.0).astype(BF16)
        back = back + jnp.dot(lhs, tiles[s], preferred_element_type=F32)
    bks[0] = back

    adds = []
    for d in range(3):
        term = ffs[d] * back
        adds.append(
            jnp.concatenate(
                [
                    jnp.sum(jnp.where(own_second, 0.0, term), axis=0, keepdims=True),
                    jnp.sum(jnp.where(own_second, term, 0.0), axis=0, keepdims=True),
                ],
                axis=1,
            )
        )
    one_down = adds[1] + ends[3, 1:2, :] * adds[0]
    cbuf[gi] = adds[2] + ends[3, 2:3, :] * one_down
    line_copies = to_all(cbuf.at[gi], cs, cr, line_peers)
    near[2] = adds[0]
    near[3] = one_down
    near_copies = [send(near.at[1 + d], near.at[d - 1], ns.at[d - 1], nr.at[d - 1], sooner[d - 1]) for d in (1, 2)]
    row_copies = [send(bks.at[0], bks.at[d], ks.at[d - 1], kr.at[d - 1], sooner[d - 1]) for d in (1, 2)]
    received(row_copies)
    rows = []
    for d in range(3):
        second = second_block(d)
        rows.append(
            jnp.concatenate([jnp.where(second, 0.0, bks[d]), jnp.where(second, bks[d], 0.0)], axis=1)
        )
    rows.append(jnp.zeros((8, RC), F32))
    first, second, third = thirds(jnp.concatenate(rows, axis=0))
    hot = sel[...].astype(BF16)
    hx[...] = (
        lax.dot_general(hot, third, TN, preferred_element_type=F32)
        + lax.dot_general(hot, second, TN, preferred_element_type=F32)
    ) + lax.dot_general(hot, first, TN, preferred_element_type=F32)

    c = jnp.zeros((CH, RC), F32)
    for i in reversed(range(ST)):
        h = hx[steps(i), :] + c
        hx[steps(i), :] = h
        c = dp[steps(i), :] * h
    for n, k in enumerate((1, 2, 4)):
        c = c + bstep[n] * jnp.where(sub8 < CH - k, pltpu.roll(c, CH - k, 0), 0.0)
    entry = jnp.where(sub8 < CH - 1, pltpu.roll(c, CH - 1, 0), 0.0)
    received(near_copies)
    close = jnp.where(tm + 1 < WINDOWS, near[0], 0.0) + jnp.where(tm + 2 < WINDOWS, near[1], 0.0)
    received(line_copies)
    run = jnp.zeros((1, RC), F32)
    for j in reversed(range(2, LINE)):
        run = abuf[j - 2] * run + cbuf[j]
    ubuf[gx, 0] = run
    ubuf[gx, 1] = cbuf[1]
    ubuf[gx, 2] = cbuf[0]
    cross_copies = to_all(ubuf.at[gx], c2s, c2r, cross_peers)
    mine = jnp.zeros((1, RC), F32)
    for j in reversed(range(3, LINE)):
        mine = jnp.where(j >= gi + 3, abuf[j - 2] * mine + cbuf[j], mine)
    received(cross_copies)
    zero = jnp.zeros((1, RC), F32)
    two, one, run = zero, zero, zero
    for j in reversed(range(1, LINES)):
        above = j > gx
        two = jnp.where(above, ubuf[j, 0] + gabuf[j, 2] * run, two)
        one = jnp.where(above, gabuf[j - 1, 3] * two + ubuf[j, 1], one)
        run = jnp.where(above, gabuf[j - 1, 4] * one + ubuf[j, 2], run)
    far = jnp.where(gi == LINE - 1, two, jnp.where(gi == LINE - 2, one, mine + ends[3, 0:1, :] * run))
    entry = entry + ends[1] * (close + far)
    for i in range(ST):
        held = hx[steps(i), :] + rp[steps(i), :] * entry
        hx[steps(i), :] = gp[steps(i), :] * held
    xb[0] = lax.dot_general(moved, hx[...].astype(BF16), TN, preferred_element_type=F32).astype(BF16)

    copies = gather_start(xb, gbs, gbr)

    gather_pass(xb, gbs, gbr, copies)
    multiply(xb, 0, True)
    received(copies[2:3])
    multiply(xb, 1, False)
    received(copies[3:4])
    multiply(xb, 3, False)
    load_res.wait()
    received(copies[4:6])
    multiply(xb, 2, False)

    image = dirv[...] + mx[...]
    imgv[...] = image
    store = pltpu.make_async_copy(imgv, img, lsem.at[12 + PIECES])
    store.start()

    def whole(x):
        return jnp.sum(jnp.sum(x, axis=0, keepdims=True), axis=1, keepdims=True)

    def inverse(x):
        ok = x > 1e-37
        return jnp.where(ok, 1.0 / jnp.where(ok, x, 1.0), 0.0)

    res = resv[...]
    largest = jnp.max(jnp.max(jnp.abs(image), axis=0, keepdims=True), axis=1, keepdims=True)
    scaled = image * inverse(largest)
    stats = jnp.where(sub == 0, whole(res * res), 0.0)
    stats = jnp.where(sub == 1, whole(dirv[...] * image), stats)
    stats = jnp.where(sub == 2, whole(res * image), stats)
    stats = jnp.where(sub == 3, whole(scaled * scaled), stats)
    stats = jnp.where(sub == 4, largest, stats)

    def merged(buf, count):
        top = buf[0, 4:5, :]
        for j in range(1, count):
            top = jnp.maximum(top, buf[j, 4:5, :])
        inv = inverse(top)
        out = jnp.zeros((8, 128), F32)
        for j in range(count):
            scale = buf[j, 4:5, :] * inv
            out = out + jnp.where(sub == 3, buf[j] * (scale * scale), buf[j])
        return jnp.where(sub == 4, top, out)

    red1[gi] = stats
    received(to_all(red1.at[gi], r1s, r1r, line_peers))
    here = gx * REGIONS + r
    red2[here] = merged(red1, LINE)
    received(to_all(red2.at[here], r2s, r2r, plane_peers))
    stats = merged(red2, LINES * REGIONS)
    norm_old = stats[0:1, :]
    alpha = norm_old / stats[1:2, :]
    reach = alpha * stats[4:5, :]
    norm_new = jnp.maximum((norm_old - 2.0 * (alpha * stats[2:3, :])) + reach * (reach * stats[3:4, :]), 0.0)
    alpha_o[...] = alpha[:, 0:1]
    beta_o[...] = (norm_new / norm_old)[:, 0:1]
    store.wait()
    for c in sent:
        c.wait_send()


def body(
    solution, residual, direction, decay, spatial, tiles,
    tile_block, tile_time, tile_cell, tile_count, noise_inv,
):
    hbm = pl.BlockSpec(memory_space=pltpu.HBM)
    vmem = pl.BlockSpec(memory_space=pltpu.VMEM)
    vector = (1, RC)
    dma = pltpu.SemaphoreType.DMA
    sems = [13 + PIECES, 6, 6, 6, 6]
    for n in (LINE - 1, LINES - 1) * 3 + (2, 2, 2, 2, 2, REGIONS - 1, LINE - 1, LINES * REGIONS - 1):
        sems += [n, n]
    image, alpha, beta = pl.pallas_call(
        kernel,
        out_shape=(
            jax.ShapeDtypeStruct((TW, RC), F32),
            jax.ShapeDtypeStruct((1, 1), F32),
            jax.ShapeDtypeStruct((1, 1), F32),
        ),
        in_specs=[hbm] * 10,
        out_specs=(hbm, vmem, vmem),
        scratch_shapes=[
            pltpu.SMEM((1, 1, SLOTS), jnp.int32),
            pltpu.SMEM((1, 1, SLOTS), jnp.int32),
            pltpu.SMEM((1, 1, SLOTS), jnp.int32),
            pltpu.SMEM((1, 1), jnp.int32),
            pltpu.VMEM((8, 128), F32),
            pltpu.VMEM((TW, RC), F32),
            pltpu.VMEM((TW, RC), F32),
            pltpu.VMEM((TW, RC), F32),
            pltpu.VMEM((PIECES, TW, 128), F32),
            pltpu.VMEM((REGIONS, RC, RC), BF16),
            pltpu.VMEM((SLOTS, 128, FB), BF16),
            pltpu.VMEM((REGIONS, TW, RC), BF16),
            pltpu.VMEM((REGIONS, TW, RC), BF16),
            pltpu.VMEM((TW, RC), F32),
            pltpu.VMEM((TW, RC), F32),
            pltpu.VMEM((TW, RC), F32),
            pltpu.VMEM((TW, RC), F32),
            pltpu.VMEM((TW, RC), F32),
            pltpu.VMEM((TW, RC), F32),
            pltpu.VMEM((3, CH, RC), F32),
            pltpu.VMEM((3, CH, RC), F32),
            pltpu.VMEM((4, CH, RC), F32),
            pltpu.VMEM((LINE,) + vector, F32),
            pltpu.VMEM((LINES, 5) + vector, F32),
            pltpu.VMEM((LINE,) + vector, F32),
            pltpu.VMEM((LINES, 3) + vector, F32),
            pltpu.VMEM((LINE,) + vector, F32),
            pltpu.VMEM((LINES, 3) + vector, F32),
            pltpu.VMEM((3, 8, 128), jnp.int32),
            pltpu.VMEM((5, 8, FB), F32),
            pltpu.VMEM((5, 8, FB), F32),
            pltpu.VMEM((3, 8, FB), F32),
            pltpu.VMEM((4,) + vector, F32),
            pltpu.VMEM((REGIONS, 8, 128), F32),
            pltpu.VMEM((LINE, 8, 128), F32),
            pltpu.VMEM((LINES * REGIONS, 8, 128), F32),
            pltpu.VMEM((32, 128), F32),
        ]
        + [dma((n,)) for n in sems],
        compiler_params=pltpu.CompilerParams(
            collective_id=0, has_side_effects=True, vmem_limit_bytes=62 << 20
        ),
        cost_estimate=pl.CostEstimate(
            flops=4 * TW * RC * RC * REGIONS, bytes_accessed=12 << 20, transcendentals=TW * RC
        ),
        name="cg_step",
    )(direction, residual, decay, spatial, tiles, tile_block, tile_time, tile_cell, tile_count, noise_inv)
    alpha = alpha[0, 0]
    beta = beta[0, 0]
    residual_new = residual - alpha * image
    return (solution + alpha * direction, residual_new, residual_new + beta * direction)


def solution(mesh):
    return jax.shard_map(
        body,
        mesh=mesh,
        in_specs=(
            P("tm", "region"),
            P("tm", "region"),
            P("tm", "region"),
            P("tm", "region"),
            P("region", None),
            P("tm", "region", None, None, None),
            P("tm", "region", None),
            P("tm", "region", None),
            P("tm", "region", None),
            P("tm", "region"),
            P("tm", None),
        ),
        out_specs=(P("tm", "region"), P("tm", "region"), P("tm", "region")),
        check_vma=False,
    )
```

```python
import jax
import jax.numpy as jnp
from jax import lax
from jax.experimental import pallas as pl
from jax.experimental.pallas import tpu as pltpu
from jax.sharding import PartitionSpec as P

MESH = pl.DeviceIdType.MESH
TW = 128
RC = 1024
FB = 512
SLOTS = 8
LINE = 16
LINES = 4
REGIONS = 4
WINDOWS = LINE * LINES
CH = 8
ST = TW // CH
PIECES = RC // 128
KQ = 256
ORDER = (0, 2, 1, 3)
CUTS = 4
DEAD = -8192
F32 = jnp.float32
BF16 = jnp.bfloat16
NT = (((1,), (1,)), ((), ()))
TN = (((0,), (0,)), ((), ()))


def kernel(
    dir_h, res_h, dec_h, spa_h, tiles_h, tblock_h, ttime_h, tcell_h, tcount_h, noise_h,
    img, ab,
    tblock, ttime, tcell, tcount, noise,
    imgv, dirv, resv, decv, spa, tiles, xa, xb, dp, gp, fp, rp, mx, hx, fstep, bstep, ends,
    abuf, gabuf, bbuf, tbuf, cbuf, ubuf, tabs, chs, ffs, bks, near, obs, red1, red2, sel,
    dsem, lsem, gas, gar, gbs, gbr, as_, ar, a2s, a2r, bs, br, b2s, b2r, cs, cr, c2s, c2r,
    ts, tr, hs, hr, fs, fr, ks, kr, ns, nr, os_, or_, r1s, r1r, r2s, r2r,
):
    tm = lax.axis_index("tm")
    r = lax.axis_index("region")
    gx = tm // LINE
    gi = lax.rem(tm, LINE)

    load_dir = {}
    for q in ORDER:
        part = slice(KQ * q, KQ * (q + 1))
        load_dir[q] = pltpu.make_async_copy(dir_h.at[:, part], dirv.at[:, part], dsem.at[q])
        load_dir[q].start()
    loads = [pltpu.make_async_copy(noise_h, noise, lsem.at[0])]
    for k in range(REGIONS):
        src = lax.rem(r + REGIONS - k, REGIONS)
        cols = pl.ds(pl.multiple_of(src * RC, RC), RC)
        loads.append(pltpu.make_async_copy(spa_h.at[:, cols], spa.at[k], lsem.at[1 + k]))
    loads.append(pltpu.make_async_copy(tiles_h.at[0, 0], tiles, lsem.at[5]))
    loads.append(pltpu.make_async_copy(res_h, resv, lsem.at[6]))
    for n in range(PIECES):
        loads.append(pltpu.make_async_copy(dec_h.at[:, 128 * n : 128 * (n + 1)], decv.at[n], lsem.at[7 + n]))
    small = ((tcount_h, tcount), (ttime_h, ttime), (tcell_h, tcell), (tblock_h, tblock))
    for n, (there, here) in enumerate(small):
        loads.append(pltpu.make_async_copy(there, here, lsem.at[7 + PIECES + n]))
    load_small = loads[7 + PIECES :] + loads[:1]
    load_spa, load_tiles, load_res, load_dec = loads[1:5], loads[5], loads[6], loads[7 : 7 + PIECES]
    for c in loads:
        c.start()

    hops = sorted(range(1, LINE), key=lambda k: -min(k, LINE - k))
    line_peers = [(gx * LINE + lax.rem(gi + k, LINE), r) for k in hops]
    cross_peers = [(lax.rem(gx + k, LINES) * LINE + gi, r) for k in range(1, LINES)]
    region_peers = [(tm, lax.rem(r + k, REGIONS)) for k in range(1, REGIONS)]
    plane_peers = [
        (lax.rem(gx + kx, LINES) * LINE + gi, lax.rem(r + ky, REGIONS))
        for kx in (2, 1, 3, 0)
        for ky in (2, 1, 3, 0)
        if kx or ky
    ]
    later = [(lax.rem(tm + d, WINDOWS), r) for d in (1, 2)]
    sooner = [(lax.rem(tm + WINDOWS - d, WINDOWS), r) for d in (1, 2)]

    barrier = pltpu.get_barrier_semaphore()
    everyone = line_peers + cross_peers + region_peers + later + sooner
    for peer in everyone:
        pl.semaphore_signal(barrier, inc=1, device_id=peer, device_id_type=MESH)

    sent = []

    def send(src, dst, ss, rs, peer):
        c = pltpu.make_async_remote_copy(
            src_ref=src, dst_ref=dst, send_sem=ss, recv_sem=rs, device_id=peer, device_id_type=MESH
        )
        c.start()
        sent.append(c)
        return c

    def to_all(ref, ss, rs, peers):
        return [send(ref, ref, ss.at[k], rs.at[k], peer) for k, peer in enumerate(peers)]

    def received(copies):
        for c in copies:
            c.wait_recv()

    sub8 = lax.broadcasted_iota(jnp.int32, (CH, RC), 0)
    sub = lax.broadcasted_iota(jnp.int32, (8, 128), 0)

    row = lax.broadcasted_iota(jnp.int32, (TW, TW), 0)
    col = lax.broadcasted_iota(jnp.int32, (TW, TW), 1)
    moved = jnp.where(lax.rem(row, CH) * ST + row // CH == col, 1.0, 0.0).astype(BF16)

    def own_part(q):
        load_dir[q].wait()
        part = dirv[:, KQ * q : KQ * (q + 1)].astype(BF16)
        xa[0, q] = jnp.dot(moved, part, preferred_element_type=F32).astype(BF16)

    own_part(ORDER[0])
    own_part(ORDER[1])
    pl.semaphore_wait(barrier, len(everyone))

    right = (tm, lax.rem(r + 1, REGIONS))
    left = (tm, lax.rem(r + REGIONS - 1, REGIONS))

    def way(q):
        return (right, 1) if q < 2 else (left, 3)

    def gather_start(x, ss, rs, make):
        copies = []
        for n, q in enumerate(ORDER):
            make(q)
            peer, slot = way(q)
            copies.append(send(x.at[0, q], x.at[slot, q], ss.at[n], rs.at[n], peer))
        for n, (peer, slot, part) in enumerate(((right, 1, pl.ds(2, 2)), (left, 3, pl.ds(0, 2)))):
            copies.append(send(x.at[0, part], x.at[slot, part], ss.at[4 + n], rs.at[4 + n], peer))
        return copies

    def gather_pass(x, ss, rs, copies):
        for n, q in enumerate(ORDER):
            peer, slot = way(q)
            copies[n].wait_recv()
            copies.append(send(x.at[slot, q], x.at[2, q], ss.at[6 + n], rs.at[6 + n], peer))

    def multiply(x, k, parts, first=False):
        def tile(n, _):
            rows = pl.ds(pl.multiple_of(n * 256, 256), 256)
            total = None
            for q in parts:
                part = lax.dot_general(
                    x[k, q], spa[k, rows, KQ * q : KQ * (q + 1)], NT, preferred_element_type=F32
                )
                total = part if total is None else total + part
            if first:
                mx[:, rows] = total
            else:
                mx[:, rows] += total
            return 0

        lax.fori_loop(0, RC // 256, tile, 0, unroll=True)

    def finish(x, copies):
        multiply(x, 0, ORDER, True)
        received(copies[4:5])
        multiply(x, 1, ORDER)
        received(copies[5:6])
        multiply(x, 3, ORDER)
        received(copies[6:8])
        multiply(x, 2, ORDER[:2])
        received(copies[8:10])
        multiply(x, 2, ORDER[2:])

    def steps(i):
        return slice(CH * i, CH * (i + 1))

    def thirds(x):
        first = x.astype(BF16)
        left_over = x - first.astype(F32)
        second = left_over.astype(BF16)
        return first, second, (left_over - second.astype(F32)).astype(BF16)

    def second_block(d):
        cell = lax.bitwise_and(tabs[d], 1) == 1
        return jnp.concatenate([cell] * (FB // 128), axis=1)

    def hand_on(dense, buf, ss, rs):
        first, second, third = thirds(dense)
        hot = sel[...].astype(BF16)
        rows = (
            jnp.dot(hot, third, preferred_element_type=F32) + jnp.dot(hot, second, preferred_element_type=F32)
        ) + jnp.dot(hot, first, preferred_element_type=F32)
        for d in range(3):
            part = rows[8 * d : 8 * d + 8, :]
            buf[2 + d if d else 0] = jnp.where(second_block(d), part[:, FB:], part[:, :FB])
        return [send(buf.at[2 + d], buf.at[d], ss.at[d - 1], rs.at[d - 1], later[d - 1]) for d in (1, 2)]

    copies = gather_start(xa, gas, gar, lambda q: own_part(q) if q in ORDER[2:] else None)

    for load in load_small:
        load.wait()
    live = sub < jnp.broadcast_to(tcount[...], (8, 128))
    table = jnp.full((8, 128), DEAD, jnp.int32)
    for s in range(SLOTS):
        table = jnp.where((sub == s) & live, ttime[0, 0, s] * 2 + tcell[0, 0, s], table)
    tabs[0] = table
    table_copies = [
        send(tabs.at[0], tabs.at[d], ts.at[d - 1], tr.at[d - 1], sooner[d - 1]) for d in (1, 2)
    ]
    for load in load_dec:
        load.wait()
    f = jnp.ones((CH, RC), F32)
    for i in range(ST):
        d = jnp.concatenate([decv[n, pl.ds(i, CH, stride=ST), :] for n in range(PIECES)], axis=1)
        dp[steps(i), :] = d
        f = f * d
        fp[steps(i), :] = f
    total = f
    for n, k in enumerate((1, 2, 4)):
        fstep[n] = f
        f = f * jnp.where(sub8 >= k, pltpu.roll(f, k, 0), 1.0)
    abuf[gi] = f[CH - 1 : CH, :]
    factor_copies = to_all(abuf.at[gi], as_, ar, line_peers)
    chunk_before = jnp.where(sub8 >= 1, pltpu.roll(f, 1, 0), 1.0)
    for i in range(ST):
        hx[steps(i), :] = fp[steps(i), :] * chunk_before
    b = total
    for n, k in enumerate((1, 2, 4)):
        bstep[n] = b
        b = b * jnp.where(sub8 < CH - k, pltpu.roll(b, CH - k, 0), 1.0)
    ends[1] = jnp.where(sub8 < CH - 1, pltpu.roll(b, CH - 1, 0), 1.0)

    received(table_copies)
    time_of = lax.broadcasted_iota(jnp.int32, (8, 128), 1)
    time_of = lax.rem(time_of, CH) * ST + time_of // CH
    for d in (1, 2):
        tabs[d] = jnp.where(tm + d < WINDOWS, tabs[d], DEAD)
    for d in range(3):
        local = lax.shift_right_arithmetic(tabs[d], 1) + (d - 2) * TW
        sel[8 * d : 8 * d + 8, :] = jnp.where(local == time_of, 1.0, 0.0)
    sel[24:32, :] = jnp.zeros((8, 128), F32)
    factor_rows = hand_on(hx[...], ffs, fs, fr)
    gather_pass(xa, gas, gar, copies)
    for load in load_spa:
        load.wait()

    received(factor_copies)
    run = jnp.ones((1, RC), F32)
    places = [run] * 3
    for j in range(LINE):
        for n in range(3):
            places[n] = jnp.where(j == gi - n, run, places[n])
        if j >= LINE - 2:
            gabuf[gx, LINE - j] = run
        run = run * abuf[j]
    gabuf[gx, 0] = run
    gabuf[gx, 3] = abuf[LINE - 1]
    gabuf[gx, 4] = abuf[LINE - 2]
    cross_copies = to_all(gabuf.at[gx], a2s, a2r, cross_peers)
    for n in range(3):
        ends[2, n : n + 1, :] = places[n]
    run = jnp.ones((1, RC), F32)
    for j in range(3, LINE):
        run = run * jnp.where(j >= gi + 3, abuf[j - 2], 1.0)
    ends[3, 0:1, :] = run
    rest = jnp.ones((CH, RC), F32)
    for i in reversed(range(ST)):
        d = dp[steps(i), :]
        gp[steps(i), :] = jnp.sqrt(1.0 - d * d)
        rp[steps(i), :] = rest
        rest = rest * d
    finish(xa, copies)

    o = jnp.zeros((CH, RC), F32)
    for i in range(ST):
        o = dp[steps(i), :] * o + gp[steps(i), :] * mx[steps(i), :]
        mx[steps(i), :] = o
    for n, k in enumerate((1, 2, 4)):
        o = o + fstep[n] * jnp.where(sub8 >= k, pltpu.roll(o, k, 0), 0.0)
    bbuf[gi] = o[CH - 1 : CH, :]
    line_copies = to_all(bbuf.at[gi], bs, br, line_peers)

    entry = jnp.where(sub8 >= 1, pltpu.roll(o, 1, 0), 0.0)
    for i in range(ST):
        mx[steps(i), :] = mx[steps(i), :] + fp[steps(i), :] * entry
    row_copies = hand_on(mx[...], chs, hs, hr)
    received(cross_copies)
    received(factor_rows)
    before = lax.rem(gx + LINES - 1, LINES)
    ends[3, 1:2, :] = jnp.where(gi >= 1, abuf[lax.rem(gi + LINE - 1, LINE)], gabuf[before, 3])
    ends[3, 2:3, :] = jnp.where(
        gi >= 2, abuf[lax.rem(gi + LINE - 2, LINE)], jnp.where(gi == 1, gabuf[before, 3], gabuf[before, 4])
    )
    received(line_copies)
    run = jnp.zeros((1, RC), F32)
    places = [run] * 3
    for j in range(LINE):
        for n in range(3):
            places[n] = jnp.where(j == gi - n, run, places[n])
        if j >= LINE - 2:
            tbuf[gx, LINE - j] = run
        run = abuf[j] * run + bbuf[j]
    tbuf[gx, 0] = run
    cross_copies = to_all(tbuf.at[gx], b2s, b2r, cross_peers)
    received(row_copies)
    received(cross_copies)
    run = jnp.zeros((1, RC), F32)
    line_before = run
    for j in range(LINES):
        line_before = jnp.where(j == gx - 1, run, line_before)
        run = jnp.where(j < gx, gabuf[j, 0] * run + tbuf[j, 0], run)
    last, last_but = [tbuf[before, n] + gabuf[before, n] * line_before for n in (1, 2)]
    inside = [places[n] + ends[2, n : n + 1, :] * run for n in range(3)]
    entering = [
        inside[0],
        jnp.where(gi >= 1, inside[1], last),
        jnp.where(gi >= 2, inside[2], jnp.where(gi == 1, last, last_but)),
    ]
    own_second = second_block(0)
    picked = jnp.zeros((8, FB), F32)
    for d in range(3):
        state = jnp.where(own_second, entering[d][:, FB:], entering[d][:, :FB])
        picked = picked + (chs[d] + ffs[d] * state)
    load_tiles.wait()

    sub_fb = lax.broadcasted_iota(jnp.int32, (8, FB), 0)
    seen = jnp.zeros((8, 128), F32)
    for s in range(SLOTS):
        lhs = jnp.where(sub_fb == tblock[0, 0, s], picked[s : s + 1, :], 0.0).astype(BF16)
        seen = seen + lax.dot_general(lhs, tiles[s], NT, preferred_element_type=F32)
    obs[r] = seen
    received(to_all(obs.at[r], os_, or_, region_peers))
    observed = ((obs[0] + obs[1]) + obs[2]) + obs[3]
    weighted = (observed * noise[...]).astype(BF16).astype(F32)

    back = jnp.zeros((8, FB), F32)
    for s in range(SLOTS):
        row = jnp.sum(jnp.where(sub == tblock[0, 0, s], weighted, 0.0), axis=0, keepdims=True)
        lhs = jnp.where((sub == s) & live, row, 0.0).astype(BF16)
        back = back + jnp.dot(lhs, tiles[s], preferred_element_type=F32)
    bks[0] = back

    adds = []
    for d in range(3):
        term = ffs[d] * back
        adds.append(
            jnp.concatenate(
                [
                    jnp.sum(jnp.where(own_second, 0.0, term), axis=0, keepdims=True),
                    jnp.sum(jnp.where(own_second, term, 0.0), axis=0, keepdims=True),
                ],
                axis=1,
            )
        )
    one_down = adds[1] + ends[3, 1:2, :] * adds[0]
    cbuf[gi] = adds[2] + ends[3, 2:3, :] * one_down
    line_copies = to_all(cbuf.at[gi], cs, cr, line_peers)
    near[2] = adds[0]
    near[3] = one_down
    near_copies = [send(near.at[1 + d], near.at[d - 1], ns.at[d - 1], nr.at[d - 1], sooner[d - 1]) for d in (1, 2)]
    row_copies = [send(bks.at[0], bks.at[d], ks.at[d - 1], kr.at[d - 1], sooner[d - 1]) for d in (1, 2)]
    received(row_copies)
    rows = []
    for d in range(3):
        second = second_block(d)
        rows.append(
            jnp.concatenate([jnp.where(second, 0.0, bks[d]), jnp.where(second, bks[d], 0.0)], axis=1)
        )
    rows.append(jnp.zeros((8, RC), F32))
    first, second, third = thirds(jnp.concatenate(rows, axis=0))
    hot = sel[...].astype(BF16)
    hx[...] = (
        lax.dot_general(hot, third, TN, preferred_element_type=F32)
        + lax.dot_general(hot, second, TN, preferred_element_type=F32)
    ) + lax.dot_general(hot, first, TN, preferred_element_type=F32)

    c = jnp.zeros((CH, RC), F32)
    for i in reversed(range(ST)):
        h = hx[steps(i), :] + c
        hx[steps(i), :] = h
        c = dp[steps(i), :] * h
    for n, k in enumerate((1, 2, 4)):
        c = c + bstep[n] * jnp.where(sub8 < CH - k, pltpu.roll(c, CH - k, 0), 0.0)
    entry = jnp.where(sub8 < CH - 1, pltpu.roll(c, CH - 1, 0), 0.0)
    received(near_copies)
    close = jnp.where(tm + 1 < WINDOWS, near[0], 0.0) + jnp.where(tm + 2 < WINDOWS, near[1], 0.0)
    received(line_copies)
    run = jnp.zeros((1, RC), F32)
    for j in reversed(range(2, LINE)):
        run = abuf[j - 2] * run + cbuf[j]
    ubuf[gx, 0] = run
    ubuf[gx, 1] = cbuf[1]
    ubuf[gx, 2] = cbuf[0]
    cross_copies = to_all(ubuf.at[gx], c2s, c2r, cross_peers)
    mine = jnp.zeros((1, RC), F32)
    for j in reversed(range(3, LINE)):
        mine = jnp.where(j >= gi + 3, abuf[j - 2] * mine + cbuf[j], mine)
    received(cross_copies)
    zero = jnp.zeros((1, RC), F32)
    two, one, run = zero, zero, zero
    for j in reversed(range(1, LINES)):
        above = j > gx
        two = jnp.where(above, ubuf[j, 0] + gabuf[j, 2] * run, two)
        one = jnp.where(above, gabuf[j - 1, 3] * two + ubuf[j, 1], one)
        run = jnp.where(above, gabuf[j - 1, 4] * one + ubuf[j, 2], run)
    far = jnp.where(gi == LINE - 1, two, jnp.where(gi == LINE - 2, one, mine + ends[3, 0:1, :] * run))
    entry = entry + ends[1] * (close + far)

    def pulled_part(q):
        part = slice(KQ * q, KQ * (q + 1))
        for i in range(ST):
            held = hx[steps(i), part] + rp[steps(i), part] * entry[:, part]
            hx[steps(i), part] = gp[steps(i), part] * held
        xb[0, q] = lax.dot_general(
            moved, hx[:, part].astype(BF16), TN, preferred_element_type=F32
        ).astype(BF16)

    copies = gather_start(xb, gbs, gbr, pulled_part)
    gather_pass(xb, gbs, gbr, copies)
    load_res.wait()
    finish(xb, copies)

    image = dirv[...] + mx[...]
    imgv[...] = image
    store = pltpu.make_async_copy(imgv, img, lsem.at[12 + PIECES])
    store.start()

    def whole(x):
        return jnp.sum(jnp.sum(x, axis=0, keepdims=True), axis=1, keepdims=True)

    def inverse(x):
        ok = x > 1e-37
        return jnp.where(ok, 1.0 / jnp.where(ok, x, 1.0), 0.0)

    res = resv[...]
    largest = jnp.max(jnp.max(jnp.abs(image), axis=0, keepdims=True), axis=1, keepdims=True)
    scaled = image * inverse(largest)
    stats = jnp.where(sub == 0, whole(res * res), 0.0)
    stats = jnp.where(sub == 1, whole(dirv[...] * image), stats)
    stats = jnp.where(sub == 2, whole(res * image), stats)
    stats = jnp.where(sub == 3, whole(scaled * scaled), stats)
    stats = jnp.where(sub == 4, largest, stats)

    def merged(buf, count):
        top = buf[0, 4:5, :]
        for j in range(1, count):
            top = jnp.maximum(top, buf[j, 4:5, :])
        inv = inverse(top)
        out = jnp.zeros((8, 128), F32)
        for j in range(count):
            scale = buf[j, 4:5, :] * inv
            out = out + jnp.where(sub == 3, buf[j] * (scale * scale), buf[j])
        return jnp.where(sub == 4, top, out)

    red1[gi] = stats
    received(to_all(red1.at[gi], r1s, r1r, line_peers))
    here = gx * REGIONS + r
    red2[here] = merged(red1, LINE)
    received(to_all(red2.at[here], r2s, r2r, plane_peers))
    stats = merged(red2, LINES * REGIONS)
    norm_old = stats[0:1, :]
    alpha = norm_old / stats[1:2, :]
    reach = alpha * stats[4:5, :]
    norm_new = jnp.maximum((norm_old - 2.0 * (alpha * stats[2:3, :])) + reach * (reach * stats[3:4, :]), 0.0)
    ab[...] = jnp.where(sub == 0, alpha, norm_new / norm_old)
    store.wait()
    for c in sent:
        c.wait_send()


def update(ab_h, img_h, dir_h, res_h, sol_h, sol_o, res_o, dir_o, ab, img, dirv, resv, sol, sn, rn, dn, asem, isem, osem):
    first = pltpu.make_async_copy(ab_h, ab, asem.at[0])
    first.start()
    loads = []
    for n in range(CUTS):
        rows = pl.ds(n * (TW // CUTS), TW // CUTS)
        loads.append(
            [
                pltpu.make_async_copy(far.at[rows], near.at[rows], isem.at[n, k])
                for k, (far, near) in enumerate(((img_h, img), (dir_h, dirv), (res_h, resv), (sol_h, sol)))
            ]
        )
        for load in loads[n]:
            load.start()
    first.wait()
    alpha, beta = ab[0:1, 0:1], ab[1:2, 0:1]
    stores = []
    for n in range(CUTS):
        rows = pl.ds(n * (TW // CUTS), TW // CUTS)
        for load in loads[n]:
            load.wait()
        left = resv[rows, :] - alpha * img[rows, :]
        rn[rows, :] = left
        sn[rows, :] = sol[rows, :] + alpha * dirv[rows, :]
        dn[rows, :] = left + beta * dirv[rows, :]
        for k, (near, far) in enumerate(((sn, sol_o), (rn, res_o), (dn, dir_o))):
            stores.append(pltpu.make_async_copy(near.at[rows], far.at[rows], osem.at[n, k]))
            stores[-1].start()
    for store in stores:
        store.wait()


def body(
    solution, residual, direction, decay, spatial, tiles,
    tile_block, tile_time, tile_cell, tile_count, noise_inv,
):
    hbm = pl.BlockSpec(memory_space=pltpu.HBM)
    vmem = pl.BlockSpec(memory_space=pltpu.VMEM)
    vector = (1, RC)
    dma = pltpu.SemaphoreType.DMA
    sems = [4, 13 + PIECES, 10, 10, 10, 10]
    for n in (LINE - 1, LINES - 1) * 3 + (2, 2, 2, 2, 2, REGIONS - 1, LINE - 1, LINES * REGIONS - 1):
        sems += [n, n]
    image, ab = pl.pallas_call(
        kernel,
        out_shape=(
            jax.ShapeDtypeStruct((TW, RC), F32),
            jax.ShapeDtypeStruct((8, 128), F32),
        ),
        in_specs=[hbm] * 10,
        out_specs=(hbm, vmem),
        scratch_shapes=[
            pltpu.SMEM((1, 1, SLOTS), jnp.int32),
            pltpu.SMEM((1, 1, SLOTS), jnp.int32),
            pltpu.SMEM((1, 1, SLOTS), jnp.int32),
            pltpu.VMEM((1, 1), jnp.int32),
            pltpu.VMEM((8, 128), F32),
            pltpu.VMEM((TW, RC), F32),
            pltpu.VMEM((TW, RC), F32),
            pltpu.VMEM((TW, RC), F32),
            pltpu.VMEM((PIECES, TW, 128), F32),
            pltpu.VMEM((REGIONS, RC, RC), BF16),
            pltpu.VMEM((SLOTS, 128, FB), BF16),
            pltpu.VMEM((REGIONS, RC // KQ, TW, KQ), BF16),
            pltpu.VMEM((REGIONS, RC // KQ, TW, KQ), BF16),
            pltpu.VMEM((TW, RC), F32),
            pltpu.VMEM((TW, RC), F32),
            pltpu.VMEM((TW, RC), F32),
            pltpu.VMEM((TW, RC), F32),
            pltpu.VMEM((TW, RC), F32),
            pltpu.VMEM((TW, RC), F32),
            pltpu.VMEM((3, CH, RC), F32),
            pltpu.VMEM((3, CH, RC), F32),
            pltpu.VMEM((4, CH, RC), F32),
            pltpu.VMEM((LINE,) + vector, F32),
            pltpu.VMEM((LINES, 5) + vector, F32),
            pltpu.VMEM((LINE,) + vector, F32),
            pltpu.VMEM((LINES, 3) + vector, F32),
            pltpu.VMEM((LINE,) + vector, F32),
            pltpu.VMEM((LINES, 3) + vector, F32),
            pltpu.VMEM((3, 8, 128), jnp.int32),
            pltpu.VMEM((5, 8, FB), F32),
            pltpu.VMEM((5, 8, FB), F32),
            pltpu.VMEM((3, 8, FB), F32),
            pltpu.VMEM((4,) + vector, F32),
            pltpu.VMEM((REGIONS, 8, 128), F32),
            pltpu.VMEM((LINE, 8, 128), F32),
            pltpu.VMEM((LINES * REGIONS, 8, 128), F32),
            pltpu.VMEM((32, 128), F32),
        ]
        + [dma((n,)) for n in sems],
        compiler_params=pltpu.CompilerParams(
            collective_id=0, has_side_effects=True, vmem_limit_bytes=62 << 20
        ),
        cost_estimate=pl.CostEstimate(
            flops=4 * TW * RC * RC * REGIONS, bytes_accessed=12 << 20, transcendentals=TW * RC
        ),
        name="cg_step",
    )(direction, residual, decay, spatial, tiles, tile_block, tile_time, tile_cell, tile_count, noise_inv)
    block = jax.ShapeDtypeStruct((TW, RC), F32)
    return pl.pallas_call(
        update,
        out_shape=(block,) * 3,
        in_specs=[hbm] * 5,
        out_specs=(hbm,) * 3,
        scratch_shapes=[pltpu.VMEM((8, 128), F32)]
        + [pltpu.VMEM((TW, RC), F32)] * 7
        + [dma((1,)), dma((CUTS, 4)), dma((CUTS, 3))],
        cost_estimate=pl.CostEstimate(flops=6 * TW * RC, bytes_accessed=28 * TW * RC, transcendentals=0),
        name="cg_update",
    )(ab, image, direction, residual, solution)


def solution(mesh):
    return jax.shard_map(
        body,
        mesh=mesh,
        in_specs=(
            P("tm", "region"),
            P("tm", "region"),
            P("tm", "region"),
            P("tm", "region"),
            P("region", None),
            P("tm", "region", None, None, None),
            P("tm", "region", None),
            P("tm", "region", None),
            P("tm", "region", None),
            P("tm", "region"),
            P("tm", None),
        ),
        out_specs=(P("tm", "region"), P("tm", "region"), P("tm", "region")),
        check_vma=False,
    )
```

```python
import jax
import jax.numpy as jnp
from jax import lax
from jax.experimental import pallas as pl
from jax.experimental.pallas import tpu as pltpu
from jax.sharding import PartitionSpec as P

MESH = pl.DeviceIdType.MESH
TW = 128
RC = 1024
FB = 512
SLOTS = 8
LINE = 16
LINES = 4
REGIONS = 4
WINDOWS = LINE * LINES
CH = 8
ST = TW // CH
PIECES = RC // 128
KQ = 256
ORDER = (0, 2, 1, 3)
CUTS = 2
DEAD = -8192
F32 = jnp.float32
BF16 = jnp.bfloat16
NT = (((1,), (1,)), ((), ()))
TN = (((0,), (0,)), ((), ()))


def kernel(
    dir_h, res_h, dec_h, spa_h, tiles_h, tblock_h, ttime_h, tcell_h, tcount_h, noise_h,
    img, ab,
    tblock, ttime, tcell, tcount, noise,
    imgv, dirv, resv, decv, spa, tiles, xa, xb, dp, gp, fp, rp, mx, hx, fstep, bstep, ends,
    abuf, gabuf, bbuf, tbuf, cbuf, ubuf, tabs, chs, ffs, bks, near, obs, red1, red2, sel,
    dsem, lsem, gas, gar, gbs, gbr, as_, ar, a2s, a2r, bs, br, b2s, b2r, cs, cr, c2s, c2r,
    ts, tr, hs, hr, fs, fr, ks, kr, ns, nr, os_, or_, r1s, r1r, r2s, r2r,
):
    tm = lax.axis_index("tm")
    r = lax.axis_index("region")
    gx = tm // LINE
    gi = lax.rem(tm, LINE)

    load_dir = {}
    for q in ORDER:
        part = slice(KQ * q, KQ * (q + 1))
        load_dir[q] = pltpu.make_async_copy(dir_h.at[:, part], dirv.at[:, part], dsem.at[q])
        load_dir[q].start()
    loads = [pltpu.make_async_copy(noise_h, noise, lsem.at[0])]
    for k in range(REGIONS):
        src = lax.rem(r + REGIONS - k, REGIONS)
        cols = pl.ds(pl.multiple_of(src * RC, RC), RC)
        loads.append(pltpu.make_async_copy(spa_h.at[:, cols], spa.at[k], lsem.at[1 + k]))
    loads.append(pltpu.make_async_copy(tiles_h.at[0, 0], tiles, lsem.at[5]))
    loads.append(pltpu.make_async_copy(res_h, resv, lsem.at[6]))
    for n in range(PIECES):
        loads.append(pltpu.make_async_copy(dec_h.at[:, 128 * n : 128 * (n + 1)], decv.at[n], lsem.at[7 + n]))
    small = ((tcount_h, tcount), (ttime_h, ttime), (tcell_h, tcell), (tblock_h, tblock))
    for n, (there, here) in enumerate(small):
        loads.append(pltpu.make_async_copy(there, here, lsem.at[7 + PIECES + n]))
    load_small = loads[7 + PIECES :] + loads[:1]
    load_spa, load_tiles, load_res, load_dec = loads[1:5], loads[5], loads[6], loads[7 : 7 + PIECES]
    for c in loads:
        c.start()

    hops = sorted(range(1, LINE), key=lambda k: -min(k, LINE - k))
    line_peers = [(gx * LINE + lax.rem(gi + k, LINE), r) for k in hops]
    cross_peers = [(lax.rem(gx + k, LINES) * LINE + gi, r) for k in range(1, LINES)]
    region_peers = [(tm, lax.rem(r + k, REGIONS)) for k in range(1, REGIONS)]
    plane_peers = [
        (lax.rem(gx + kx, LINES) * LINE + gi, lax.rem(r + ky, REGIONS))
        for kx in (2, 1, 3, 0)
        for ky in (2, 1, 3, 0)
        if kx or ky
    ]
    later = [(lax.rem(tm + d, WINDOWS), r) for d in (1, 2)]
    sooner = [(lax.rem(tm + WINDOWS - d, WINDOWS), r) for d in (1, 2)]

    barrier = pltpu.get_barrier_semaphore()
    everyone = line_peers + cross_peers + region_peers + later + sooner
    for peer in everyone:
        pl.semaphore_signal(barrier, inc=1, device_id=peer, device_id_type=MESH)

    sent = []

    def send(src, dst, ss, rs, peer):
        c = pltpu.make_async_remote_copy(
            src_ref=src, dst_ref=dst, send_sem=ss, recv_sem=rs, device_id=peer, device_id_type=MESH
        )
        c.start()
        sent.append(c)
        return c

    def to_all(ref, ss, rs, peers):
        return [send(ref, ref, ss.at[k], rs.at[k], peer) for k, peer in enumerate(peers)]

    def received(copies):
        for c in copies:
            c.wait_recv()

    sub8 = lax.broadcasted_iota(jnp.int32, (CH, RC), 0)
    sub = lax.broadcasted_iota(jnp.int32, (8, 128), 0)

    row = lax.broadcasted_iota(jnp.int32, (TW, TW), 0)
    col = lax.broadcasted_iota(jnp.int32, (TW, TW), 1)
    moved = jnp.where(lax.rem(row, CH) * ST + row // CH == col, 1.0, 0.0).astype(BF16)

    def own_part(q):
        load_dir[q].wait()
        part = dirv[:, KQ * q : KQ * (q + 1)].astype(BF16)
        xa[0, q] = jnp.dot(moved, part, preferred_element_type=F32).astype(BF16)

    own_part(ORDER[0])
    own_part(ORDER[1])
    pl.semaphore_wait(barrier, len(everyone))

    right = (tm, lax.rem(r + 1, REGIONS))
    left = (tm, lax.rem(r + REGIONS - 1, REGIONS))

    def way(q):
        return (right, 1) if q < 2 else (left, 3)

    def gather_start(x, ss, rs, make):
        copies = []
        for n, q in enumerate(ORDER):
            make(q)
            peer, slot = way(q)
            copies.append(send(x.at[0, q], x.at[slot, q], ss.at[n], rs.at[n], peer))
        for n, (peer, slot, part) in enumerate(((right, 1, pl.ds(2, 2)), (left, 3, pl.ds(0, 2)))):
            copies.append(send(x.at[0, part], x.at[slot, part], ss.at[4 + n], rs.at[4 + n], peer))
        return copies

    def gather_pass(x, ss, rs, copies):
        for n, q in enumerate(ORDER):
            peer, slot = way(q)
            copies[n].wait_recv()
            copies.append(send(x.at[slot, q], x.at[2, q], ss.at[6 + n], rs.at[6 + n], peer))

    def multiply(x, k, parts, first=False):
        def tile(n, _):
            rows = pl.ds(pl.multiple_of(n * 256, 256), 256)
            total = None
            for q in parts:
                part = lax.dot_general(
                    x[k, q], spa[k, rows, KQ * q : KQ * (q + 1)], NT, preferred_element_type=F32
                )
                total = part if total is None else total + part
            if first:
                mx[:, rows] = total
            else:
                mx[:, rows] += total
            return 0

        lax.fori_loop(0, RC // 256, tile, 0, unroll=True)

    def finish(x, copies):
        multiply(x, 0, ORDER, True)
        received(copies[4:5])
        multiply(x, 1, ORDER)
        received(copies[5:6])
        multiply(x, 3, ORDER)
        received(copies[6:8])
        multiply(x, 2, ORDER[:2])
        received(copies[8:10])
        multiply(x, 2, ORDER[2:])

    def steps(i):
        return slice(CH * i, CH * (i + 1))

    def thirds(x):
        first = x.astype(BF16)
        left_over = x - first.astype(F32)
        second = left_over.astype(BF16)
        return first, second, (left_over - second.astype(F32)).astype(BF16)

    def whole(x):
        return jnp.sum(jnp.sum(x, axis=0, keepdims=True), axis=1, keepdims=True)

    def second_block(d):
        cell = lax.bitwise_and(tabs[d], 1) == 1
        return jnp.concatenate([cell] * (FB // 128), axis=1)

    def hand_on(dense, buf, ss, rs):
        first, second, third = thirds(dense)
        hot = sel[...].astype(BF16)
        rows = (
            jnp.dot(hot, third, preferred_element_type=F32) + jnp.dot(hot, second, preferred_element_type=F32)
        ) + jnp.dot(hot, first, preferred_element_type=F32)
        for d in range(3):
            part = rows[8 * d : 8 * d + 8, :]
            buf[2 + d if d else 0] = jnp.where(second_block(d), part[:, FB:], part[:, :FB])
        return [send(buf.at[2 + d], buf.at[d], ss.at[d - 1], rs.at[d - 1], later[d - 1]) for d in (1, 2)]

    copies = gather_start(xa, gas, gar, lambda q: own_part(q) if q in ORDER[2:] else None)

    for load in load_small:
        load.wait()
    live = sub < jnp.broadcast_to(tcount[...], (8, 128))
    table = jnp.full((8, 128), DEAD, jnp.int32)
    for s in range(SLOTS):
        table = jnp.where((sub == s) & live, ttime[0, 0, s] * 2 + tcell[0, 0, s], table)
    tabs[0] = table
    table_copies = [
        send(tabs.at[0], tabs.at[d], ts.at[d - 1], tr.at[d - 1], sooner[d - 1]) for d in (1, 2)
    ]
    for load in load_dec:
        load.wait()
    f = jnp.ones((CH, RC), F32)
    for i in range(ST):
        d = jnp.concatenate([decv[n, pl.ds(i, CH, stride=ST), :] for n in range(PIECES)], axis=1)
        dp[steps(i), :] = d
        f = f * d
        fp[steps(i), :] = f
    total = f
    for n, k in enumerate((1, 2, 4)):
        fstep[n] = f
        f = f * jnp.where(sub8 >= k, pltpu.roll(f, k, 0), 1.0)
    abuf[gi] = f[CH - 1 : CH, :]
    factor_copies = to_all(abuf.at[gi], as_, ar, line_peers)
    chunk_before = jnp.where(sub8 >= 1, pltpu.roll(f, 1, 0), 1.0)
    for i in range(ST):
        hx[steps(i), :] = fp[steps(i), :] * chunk_before
    b = total
    for n, k in enumerate((1, 2, 4)):
        bstep[n] = b
        b = b * jnp.where(sub8 < CH - k, pltpu.roll(b, CH - k, 0), 1.0)
    ends[1] = jnp.where(sub8 < CH - 1, pltpu.roll(b, CH - 1, 0), 1.0)

    gather_pass(xa, gas, gar, copies)

    received(table_copies)
    time_of = lax.broadcasted_iota(jnp.int32, (8, 128), 1)
    time_of = lax.rem(time_of, CH) * ST + time_of // CH
    for d in (1, 2):
        tabs[d] = jnp.where(tm + d < WINDOWS, tabs[d], DEAD)
    for d in range(3):
        local = lax.shift_right_arithmetic(tabs[d], 1) + (d - 2) * TW
        sel[8 * d : 8 * d + 8, :] = jnp.where(local == time_of, 1.0, 0.0)
    sel[24:32, :] = jnp.zeros((8, 128), F32)
    factor_rows = hand_on(hx[...], ffs, fs, fr)
    for load in load_spa:
        load.wait()

    received(factor_copies)
    run = jnp.ones((1, RC), F32)
    places = [run] * 3
    for j in range(LINE):
        for n in range(3):
            places[n] = jnp.where(j == gi - n, run, places[n])
        if j >= LINE - 2:
            gabuf[gx, LINE - j] = run
        run = run * abuf[j]
    gabuf[gx, 0] = run
    gabuf[gx, 3] = abuf[LINE - 1]
    gabuf[gx, 4] = abuf[LINE - 2]
    cross_copies = to_all(gabuf.at[gx], a2s, a2r, cross_peers)
    for n in range(3):
        ends[2, n : n + 1, :] = places[n]
    run = jnp.ones((1, RC), F32)
    for j in range(3, LINE):
        run = run * jnp.where(j >= gi + 3, abuf[j - 2], 1.0)
    ends[3, 0:1, :] = run
    rest = jnp.ones((CH, RC), F32)
    for i in reversed(range(ST)):
        d = dp[steps(i), :]
        gp[steps(i), :] = jnp.sqrt(1.0 - d * d)
        rp[steps(i), :] = rest
        rest = rest * d
    finish(xa, copies)

    o = jnp.zeros((CH, RC), F32)
    for i in range(ST):
        o = dp[steps(i), :] * o + gp[steps(i), :] * mx[steps(i), :]
        mx[steps(i), :] = o
    for n, k in enumerate((1, 2, 4)):
        o = o + fstep[n] * jnp.where(sub8 >= k, pltpu.roll(o, k, 0), 0.0)
    bbuf[gi] = o[CH - 1 : CH, :]
    line_copies = to_all(bbuf.at[gi], bs, br, line_peers)

    entry = jnp.where(sub8 >= 1, pltpu.roll(o, 1, 0), 0.0)
    for i in range(ST):
        mx[steps(i), :] = mx[steps(i), :] + fp[steps(i), :] * entry
    row_copies = hand_on(mx[...], chs, hs, hr)
    received(cross_copies)
    received(factor_rows)
    before = lax.rem(gx + LINES - 1, LINES)
    ends[3, 1:2, :] = jnp.where(gi >= 1, abuf[lax.rem(gi + LINE - 1, LINE)], gabuf[before, 3])
    ends[3, 2:3, :] = jnp.where(
        gi >= 2, abuf[lax.rem(gi + LINE - 2, LINE)], jnp.where(gi == 1, gabuf[before, 3], gabuf[before, 4])
    )
    received(line_copies)
    run = jnp.zeros((1, RC), F32)
    places = [run] * 3
    for j in range(LINE):
        for n in range(3):
            places[n] = jnp.where(j == gi - n, run, places[n])
        if j >= LINE - 2:
            tbuf[gx, LINE - j] = run
        run = abuf[j] * run + bbuf[j]
    tbuf[gx, 0] = run
    cross_copies = to_all(tbuf.at[gx], b2s, b2r, cross_peers)
    received(row_copies)
    received(cross_copies)
    run = jnp.zeros((1, RC), F32)
    line_before = run
    for j in range(LINES):
        line_before = jnp.where(j == gx - 1, run, line_before)
        run = jnp.where(j < gx, gabuf[j, 0] * run + tbuf[j, 0], run)
    last, last_but = [tbuf[before, n] + gabuf[before, n] * line_before for n in (1, 2)]
    inside = [places[n] + ends[2, n : n + 1, :] * run for n in range(3)]
    entering = [
        inside[0],
        jnp.where(gi >= 1, inside[1], last),
        jnp.where(gi >= 2, inside[2], jnp.where(gi == 1, last, last_but)),
    ]
    own_second = second_block(0)
    picked = jnp.zeros((8, FB), F32)
    for d in range(3):
        state = jnp.where(own_second, entering[d][:, FB:], entering[d][:, :FB])
        picked = picked + (chs[d] + ffs[d] * state)
    load_tiles.wait()

    sub_fb = lax.broadcasted_iota(jnp.int32, (8, FB), 0)
    seen = jnp.zeros((8, 128), F32)
    for s in range(SLOTS):
        lhs = jnp.where(sub_fb == tblock[0, 0, s], picked[s : s + 1, :], 0.0).astype(BF16)
        seen = seen + lax.dot_general(lhs, tiles[s], NT, preferred_element_type=F32)
    obs[r] = seen
    received(to_all(obs.at[r], os_, or_, region_peers))
    observed = ((obs[0] + obs[1]) + obs[2]) + obs[3]
    weighted = (observed * noise[...]).astype(BF16).astype(F32)

    back = jnp.zeros((8, FB), F32)
    for s in range(SLOTS):
        row = jnp.sum(jnp.where(sub == tblock[0, 0, s], weighted, 0.0), axis=0, keepdims=True)
        lhs = jnp.where((sub == s) & live, row, 0.0).astype(BF16)
        back = back + jnp.dot(lhs, tiles[s], preferred_element_type=F32)
    bks[0] = back

    adds = []
    for d in range(3):
        term = ffs[d] * back
        adds.append(
            jnp.concatenate(
                [
                    jnp.sum(jnp.where(own_second, 0.0, term), axis=0, keepdims=True),
                    jnp.sum(jnp.where(own_second, term, 0.0), axis=0, keepdims=True),
                ],
                axis=1,
            )
        )
    one_down = adds[1] + ends[3, 1:2, :] * adds[0]
    cbuf[gi] = adds[2] + ends[3, 2:3, :] * one_down
    line_copies = to_all(cbuf.at[gi], cs, cr, line_peers)
    near[2] = adds[0]
    near[3] = one_down
    near_copies = [send(near.at[1 + d], near.at[d - 1], ns.at[d - 1], nr.at[d - 1], sooner[d - 1]) for d in (1, 2)]
    row_copies = [send(bks.at[0], bks.at[d], ks.at[d - 1], kr.at[d - 1], sooner[d - 1]) for d in (1, 2)]
    received(row_copies)
    rows = []
    for d in range(3):
        second = second_block(d)
        rows.append(
            jnp.concatenate([jnp.where(second, 0.0, bks[d]), jnp.where(second, bks[d], 0.0)], axis=1)
        )
    rows.append(jnp.zeros((8, RC), F32))
    first, second, third = thirds(jnp.concatenate(rows, axis=0))
    hot = sel[...].astype(BF16)
    hx[...] = (
        lax.dot_general(hot, third, TN, preferred_element_type=F32)
        + lax.dot_general(hot, second, TN, preferred_element_type=F32)
    ) + lax.dot_general(hot, first, TN, preferred_element_type=F32)

    c = jnp.zeros((CH, RC), F32)
    for i in reversed(range(ST)):
        h = hx[steps(i), :] + c
        hx[steps(i), :] = h
        c = dp[steps(i), :] * h
    for n, k in enumerate((1, 2, 4)):
        c = c + bstep[n] * jnp.where(sub8 < CH - k, pltpu.roll(c, CH - k, 0), 0.0)
    entry = jnp.where(sub8 < CH - 1, pltpu.roll(c, CH - 1, 0), 0.0)
    received(near_copies)
    close = jnp.where(tm + 1 < WINDOWS, near[0], 0.0) + jnp.where(tm + 2 < WINDOWS, near[1], 0.0)
    received(line_copies)
    run = jnp.zeros((1, RC), F32)
    for j in reversed(range(2, LINE)):
        run = abuf[j - 2] * run + cbuf[j]
    ubuf[gx, 0] = run
    ubuf[gx, 1] = cbuf[1]
    ubuf[gx, 2] = cbuf[0]
    cross_copies = to_all(ubuf.at[gx], c2s, c2r, cross_peers)
    mine = jnp.zeros((1, RC), F32)
    for j in reversed(range(3, LINE)):
        mine = jnp.where(j >= gi + 3, abuf[j - 2] * mine + cbuf[j], mine)
    received(cross_copies)
    zero = jnp.zeros((1, RC), F32)
    two, one, run = zero, zero, zero
    for j in reversed(range(1, LINES)):
        above = j > gx
        two = jnp.where(above, ubuf[j, 0] + gabuf[j, 2] * run, two)
        one = jnp.where(above, gabuf[j - 1, 3] * two + ubuf[j, 1], one)
        run = jnp.where(above, gabuf[j - 1, 4] * one + ubuf[j, 2], run)
    far = jnp.where(gi == LINE - 1, two, jnp.where(gi == LINE - 2, one, mine + ends[3, 0:1, :] * run))
    entry = entry + ends[1] * (close + far)

    def pulled_part(q):
        part = slice(KQ * q, KQ * (q + 1))
        for i in range(ST):
            held = hx[steps(i), part] + rp[steps(i), part] * entry[:, part]
            hx[steps(i), part] = gp[steps(i), part] * held
        xb[0, q] = lax.dot_general(
            moved, hx[:, part].astype(BF16), TN, preferred_element_type=F32
        ).astype(BF16)

    copies = gather_start(xb, gbs, gbr, pulled_part)
    gather_pass(xb, gbs, gbr, copies)
    load_res.wait()
    res = resv[...]
    norm_here = whole(res * res)
    finish(xb, copies)

    image = dirv[...] + mx[...]
    imgv[...] = image
    store = pltpu.make_async_copy(imgv, img, lsem.at[12 + PIECES])
    store.start()

    def inverse(x):
        ok = x > 1e-37
        return jnp.where(ok, 1.0 / jnp.where(ok, x, 1.0), 0.0)

    res = resv[...]
    largest = jnp.max(jnp.max(jnp.abs(image), axis=0, keepdims=True), axis=1, keepdims=True)
    scaled = image * inverse(largest)
    stats = jnp.where(sub == 0, norm_here, 0.0)
    stats = jnp.where(sub == 1, whole(dirv[...] * image), stats)
    stats = jnp.where(sub == 2, whole(res * image), stats)
    stats = jnp.where(sub == 3, whole(scaled * scaled), stats)
    stats = jnp.where(sub == 4, largest, stats)

    def merged(buf, count):
        top = buf[0, 4:5, :]
        for j in range(1, count):
            top = jnp.maximum(top, buf[j, 4:5, :])
        inv = inverse(top)
        out = jnp.zeros((8, 128), F32)
        for j in range(count):
            scale = buf[j, 4:5, :] * inv
            out = out + jnp.where(sub == 3, buf[j] * (scale * scale), buf[j])
        return jnp.where(sub == 4, top, out)

    red1[gi] = stats
    older = list(sent)
    copies = to_all(red1.at[gi], r1s, r1r, line_peers)
    for c in older:
        c.wait_send()
    received(copies)
    here = gx * REGIONS + r
    store.wait()
    red2[here] = merged(red1, LINE)
    received(to_all(red2.at[here], r2s, r2r, plane_peers))
    stats = merged(red2, LINES * REGIONS)
    norm_old = stats[0:1, :]
    alpha = norm_old / stats[1:2, :]
    reach = alpha * stats[4:5, :]
    norm_new = jnp.maximum((norm_old - 2.0 * (alpha * stats[2:3, :])) + reach * (reach * stats[3:4, :]), 0.0)
    ab[...] = jnp.where(sub == 0, alpha, norm_new / norm_old)
    for c in sent[len(older) :]:
        c.wait_send()


def update(ab_h, img_h, dir_h, res_h, sol_h, sol_o, res_o, dir_o, ab, img, dirv, resv, sol, sn, rn, dn, asem, isem, osem):
    first = pltpu.make_async_copy(ab_h, ab, asem.at[0])
    first.start()
    loads = []
    for n in range(CUTS):
        rows = pl.ds(n * (TW // CUTS), TW // CUTS)
        loads.append(
            [
                pltpu.make_async_copy(far.at[rows], near.at[rows], isem.at[n, k])
                for k, (far, near) in enumerate(((img_h, img), (dir_h, dirv), (res_h, resv), (sol_h, sol)))
            ]
        )
        for load in loads[n]:
            load.start()
    first.wait()
    alpha, beta = ab[0:1, 0:1], ab[1:2, 0:1]
    stores = []
    for n in range(CUTS):
        rows = pl.ds(n * (TW // CUTS), TW // CUTS)
        for load in loads[n]:
            load.wait()
        left = resv[rows, :] - alpha * img[rows, :]
        rn[rows, :] = left
        sn[rows, :] = sol[rows, :] + alpha * dirv[rows, :]
        dn[rows, :] = left + beta * dirv[rows, :]
        for k, (near, far) in enumerate(((sn, sol_o), (rn, res_o), (dn, dir_o))):
            stores.append(pltpu.make_async_copy(near.at[rows], far.at[rows], osem.at[n, k]))
            stores[-1].start()
    for store in stores:
        store.wait()


def body(
    solution, residual, direction, decay, spatial, tiles,
    tile_block, tile_time, tile_cell, tile_count, noise_inv,
):
    hbm = pl.BlockSpec(memory_space=pltpu.HBM)
    vmem = pl.BlockSpec(memory_space=pltpu.VMEM)
    vector = (1, RC)
    dma = pltpu.SemaphoreType.DMA
    sems = [4, 13 + PIECES, 10, 10, 10, 10]
    for n in (LINE - 1, LINES - 1) * 3 + (2, 2, 2, 2, 2, REGIONS - 1, LINE - 1, LINES * REGIONS - 1):
        sems += [n, n]
    image, ab = pl.pallas_call(
        kernel,
        out_shape=(
            jax.ShapeDtypeStruct((TW, RC), F32),
            jax.ShapeDtypeStruct((8, 128), F32),
        ),
        in_specs=[hbm] * 10,
        out_specs=(hbm, vmem),
        scratch_shapes=[
            pltpu.SMEM((1, 1, SLOTS), jnp.int32),
            pltpu.SMEM((1, 1, SLOTS), jnp.int32),
            pltpu.SMEM((1, 1, SLOTS), jnp.int32),
            pltpu.VMEM((1, 1), jnp.int32),
            pltpu.VMEM((8, 128), F32),
            pltpu.VMEM((TW, RC), F32),
            pltpu.VMEM((TW, RC), F32),
            pltpu.VMEM((TW, RC), F32),
            pltpu.VMEM((PIECES, TW, 128), F32),
            pltpu.VMEM((REGIONS, RC, RC), BF16),
            pltpu.VMEM((SLOTS, 128, FB), BF16),
            pltpu.VMEM((REGIONS, RC // KQ, TW, KQ), BF16),
            pltpu.VMEM((REGIONS, RC // KQ, TW, KQ), BF16),
            pltpu.VMEM((TW, RC), F32),
            pltpu.VMEM((TW, RC), F32),
            pltpu.VMEM((TW, RC), F32),
            pltpu.VMEM((TW, RC), F32),
            pltpu.VMEM((TW, RC), F32),
            pltpu.VMEM((TW, RC), F32),
            pltpu.VMEM((3, CH, RC), F32),
            pltpu.VMEM((3, CH, RC), F32),
            pltpu.VMEM((4, CH, RC), F32),
            pltpu.VMEM((LINE,) + vector, F32),
            pltpu.VMEM((LINES, 5) + vector, F32),
            pltpu.VMEM((LINE,) + vector, F32),
            pltpu.VMEM((LINES, 3) + vector, F32),
            pltpu.VMEM((LINE,) + vector, F32),
            pltpu.VMEM((LINES, 3) + vector, F32),
            pltpu.VMEM((3, 8, 128), jnp.int32),
            pltpu.VMEM((5, 8, FB), F32),
            pltpu.VMEM((5, 8, FB), F32),
            pltpu.VMEM((3, 8, FB), F32),
            pltpu.VMEM((4,) + vector, F32),
            pltpu.VMEM((REGIONS, 8, 128), F32),
            pltpu.VMEM((LINE, 8, 128), F32),
            pltpu.VMEM((LINES * REGIONS, 8, 128), F32),
            pltpu.VMEM((32, 128), F32),
        ]
        + [dma((n,)) for n in sems],
        compiler_params=pltpu.CompilerParams(
            collective_id=0, has_side_effects=True, vmem_limit_bytes=62 << 20
        ),
        cost_estimate=pl.CostEstimate(
            flops=4 * TW * RC * RC * REGIONS, bytes_accessed=12 << 20, transcendentals=TW * RC
        ),
        name="cg_step",
    )(direction, residual, decay, spatial, tiles, tile_block, tile_time, tile_cell, tile_count, noise_inv)
    block = jax.ShapeDtypeStruct((TW, RC), F32)
    return pl.pallas_call(
        update,
        out_shape=(block,) * 3,
        in_specs=[hbm] * 5,
        out_specs=(hbm,) * 3,
        scratch_shapes=[pltpu.VMEM((8, 128), F32)]
        + [pltpu.VMEM((TW, RC), F32)] * 7
        + [dma((1,)), dma((CUTS, 4)), dma((CUTS, 3))],
        cost_estimate=pl.CostEstimate(flops=6 * TW * RC, bytes_accessed=28 * TW * RC, transcendentals=0),
        name="cg_update",
    )(ab, image, direction, residual, solution)


def solution(mesh):
    return jax.shard_map(
        body,
        mesh=mesh,
        in_specs=(
            P("tm", "region"),
            P("tm", "region"),
            P("tm", "region"),
            P("tm", "region"),
            P("region", None),
            P("tm", "region", None, None, None),
            P("tm", "region", None),
            P("tm", "region", None),
            P("tm", "region", None),
            P("tm", "region"),
            P("tm", None),
        ),
        out_specs=(P("tm", "region"), P("tm", "region"), P("tm", "region")),
        check_vma=False,
    )
```

```python
import jax
import jax.numpy as jnp
from jax import lax
from jax.experimental import pallas as pl
from jax.experimental.pallas import tpu as pltpu
from jax.sharding import PartitionSpec as P

MESH = pl.DeviceIdType.MESH
TW = 128
RC = 1024
FB = 512
SLOTS = 8
LINE = 16
LINES = 4
REGIONS = 4
WINDOWS = LINE * LINES
CH = 8
ST = TW // CH
PIECES = RC // 128
KQ = 256
ORDER = (0, 2, 1, 3)
CUTS = 2
DEAD = -8192
F32 = jnp.float32
BF16 = jnp.bfloat16
NT = (((1,), (1,)), ((), ()))
TN = (((0,), (0,)), ((), ()))


def kernel(
    dir_h, res_h, dec_h, spa_h, tiles_h, tblock_h, ttime_h, tcell_h, tcount_h, noise_h,
    img, ab,
    tblock, ttime, tcell, tcount, noise,
    imgv, dirv, resv, decv, spa, tiles, xa, xb, dp, gp, fp, rp, mx, hx, fstep, bstep, ends,
    abuf, gabuf, bbuf, tbuf, cbuf, ubuf, tabs, chs, ffs, bks, near, obs, red1, red2, sel,
    dsem, lsem, gas, gar, gbs, gbr, as_, ar, a2s, a2r, bs, br, b2s, b2r, cs, cr, c2s, c2r,
    ts, tr, hs, hr, fs, fr, ks, kr, ns, nr, os_, or_, r1s, r1r, r2s, r2r,
):
    tm = lax.axis_index("tm")
    r = lax.axis_index("region")
    gx = tm // LINE
    gi = lax.rem(tm, LINE)

    load_dir = {}
    for q in ORDER:
        part = slice(KQ * q, KQ * (q + 1))
        load_dir[q] = pltpu.make_async_copy(dir_h.at[:, part], dirv.at[:, part], dsem.at[q])
        load_dir[q].start()
    loads = [pltpu.make_async_copy(noise_h, noise, lsem.at[0])]
    for k in range(REGIONS):
        src = lax.rem(r + REGIONS - k, REGIONS)
        cols = pl.ds(pl.multiple_of(src * RC, RC), RC)
        loads.append(pltpu.make_async_copy(spa_h.at[:, cols], spa.at[k], lsem.at[1 + k]))
    loads.append(pltpu.make_async_copy(tiles_h.at[0, 0], tiles, lsem.at[5]))
    loads.append(pltpu.make_async_copy(res_h, resv, lsem.at[6]))
    for n in range(PIECES):
        loads.append(pltpu.make_async_copy(dec_h.at[:, 128 * n : 128 * (n + 1)], decv.at[n], lsem.at[7 + n]))
    small = ((tcount_h, tcount), (ttime_h, ttime), (tcell_h, tcell), (tblock_h, tblock))
    for n, (there, here) in enumerate(small):
        loads.append(pltpu.make_async_copy(there, here, lsem.at[7 + PIECES + n]))
    load_small = loads[7 + PIECES :] + loads[:1]
    load_spa, load_tiles, load_res, load_dec = loads[1:5], loads[5], loads[6], loads[7 : 7 + PIECES]
    for c in loads:
        c.start()

    hops = sorted(range(1, LINE), key=lambda k: -min(k, LINE - k))
    line_peers = [(gx * LINE + lax.rem(gi + k, LINE), r) for k in hops]
    cross_peers = [(lax.rem(gx + k, LINES) * LINE + gi, r) for k in range(1, LINES)]
    region_peers = [(tm, lax.rem(r + k, REGIONS)) for k in range(1, REGIONS)]
    plane_peers = [
        (lax.rem(gx + kx, LINES) * LINE + gi, lax.rem(r + ky, REGIONS))
        for kx in (2, 1, 3, 0)
        for ky in (2, 1, 3, 0)
        if kx or ky
    ]
    later = [(lax.rem(tm + d, WINDOWS), r) for d in (1, 2)]
    sooner = [(lax.rem(tm + WINDOWS - d, WINDOWS), r) for d in (1, 2)]

    barrier = pltpu.get_barrier_semaphore()
    everyone = line_peers + cross_peers + region_peers + later + sooner
    for peer in everyone:
        pl.semaphore_signal(barrier, inc=1, device_id=peer, device_id_type=MESH)

    sent = []

    def send(src, dst, ss, rs, peer):
        c = pltpu.make_async_remote_copy(
            src_ref=src, dst_ref=dst, send_sem=ss, recv_sem=rs, device_id=peer, device_id_type=MESH
        )
        c.start()
        sent.append(c)
        return c

    def to_all(ref, ss, rs, peers):
        return [send(ref, ref, ss.at[k], rs.at[k], peer) for k, peer in enumerate(peers)]

    def received(copies):
        for c in copies:
            c.wait_recv()

    sub8 = lax.broadcasted_iota(jnp.int32, (CH, RC), 0)
    sub = lax.broadcasted_iota(jnp.int32, (8, 128), 0)

    row = lax.broadcasted_iota(jnp.int32, (TW, TW), 0)
    col = lax.broadcasted_iota(jnp.int32, (TW, TW), 1)
    moved = jnp.where(lax.rem(row, CH) * ST + row // CH == col, 1.0, 0.0).astype(BF16)

    def own_part(q):
        load_dir[q].wait()
        part = dirv[:, KQ * q : KQ * (q + 1)].astype(BF16)
        xa[0, q] = jnp.dot(moved, part, preferred_element_type=F32).astype(BF16)

    own_part(ORDER[0])
    own_part(ORDER[1])
    pl.semaphore_wait(barrier, len(everyone))

    right = (tm, lax.rem(r + 1, REGIONS))
    left = (tm, lax.rem(r + REGIONS - 1, REGIONS))

    def way(q):
        return (right, 1) if q < 2 else (left, 3)

    def gather_start(x, ss, rs, make):
        copies = []
        for n, q in enumerate(ORDER):
            make(q)
            peer, slot = way(q)
            copies.append(send(x.at[0, q], x.at[slot, q], ss.at[n], rs.at[n], peer))
        for n, (peer, slot, part) in enumerate(((right, 1, pl.ds(2, 2)), (left, 3, pl.ds(0, 2)))):
            copies.append(send(x.at[0, part], x.at[slot, part], ss.at[4 + n], rs.at[4 + n], peer))
        return copies

    def gather_pass(x, ss, rs, copies):
        for n, q in enumerate(ORDER):
            peer, slot = way(q)
            copies[n].wait_recv()
            copies.append(send(x.at[slot, q], x.at[2, q], ss.at[6 + n], rs.at[6 + n], peer))

    def multiply(x, k, parts, first=False):
        def tile(n, _):
            rows = pl.ds(pl.multiple_of(n * 256, 256), 256)
            total = None
            for q in parts:
                part = lax.dot_general(
                    x[k, q], spa[k, rows, KQ * q : KQ * (q + 1)], NT, preferred_element_type=F32
                )
                total = part if total is None else total + part
            if first:
                mx[:, rows] = total
            else:
                mx[:, rows] += total
            return 0

        lax.fori_loop(0, RC // 256, tile, 0, unroll=True)

    def finish(x, copies, between=lambda: None):
        received(copies[4:5])
        multiply(x, 1, ORDER)
        received(copies[5:6])
        multiply(x, 3, ORDER)
        between()
        received(copies[6:8])
        multiply(x, 2, ORDER[:2])
        received(copies[8:10])
        multiply(x, 2, ORDER[2:])

    def steps(i):
        return slice(CH * i, CH * (i + 1))

    def thirds(x):
        first = x.astype(BF16)
        left_over = x - first.astype(F32)
        second = left_over.astype(BF16)
        return first, second, (left_over - second.astype(F32)).astype(BF16)

    def whole(x):
        return jnp.sum(jnp.sum(x, axis=0, keepdims=True), axis=1, keepdims=True)

    def second_block(d):
        cell = lax.bitwise_and(tabs[d], 1) == 1
        return jnp.concatenate([cell] * (FB // 128), axis=1)

    def hand_on(dense, buf, ss, rs):
        first, second, third = thirds(dense)
        hot = sel[...].astype(BF16)
        rows = (
            jnp.dot(hot, third, preferred_element_type=F32) + jnp.dot(hot, second, preferred_element_type=F32)
        ) + jnp.dot(hot, first, preferred_element_type=F32)
        for d in range(3):
            part = rows[8 * d : 8 * d + 8, :]
            buf[2 + d if d else 0] = jnp.where(second_block(d), part[:, FB:], part[:, :FB])
        return [send(buf.at[2 + d], buf.at[d], ss.at[d - 1], rs.at[d - 1], later[d - 1]) for d in (1, 2)]

    copies = gather_start(xa, gas, gar, lambda q: own_part(q) if q in ORDER[2:] else None)

    for load in load_small:
        load.wait()
    live = sub < jnp.broadcast_to(tcount[...], (8, 128))
    table = jnp.full((8, 128), DEAD, jnp.int32)
    for s in range(SLOTS):
        table = jnp.where((sub == s) & live, ttime[0, 0, s] * 2 + tcell[0, 0, s], table)
    tabs[0] = table
    table_copies = [
        send(tabs.at[0], tabs.at[d], ts.at[d - 1], tr.at[d - 1], sooner[d - 1]) for d in (1, 2)
    ]
    for load in load_dec:
        load.wait()
    f = jnp.ones((CH, RC), F32)
    for i in range(ST):
        d = jnp.concatenate([decv[n, pl.ds(i, CH, stride=ST), :] for n in range(PIECES)], axis=1)
        dp[steps(i), :] = d
        f = f * d
        fp[steps(i), :] = f
    total = f
    for n, k in enumerate((1, 2, 4)):
        fstep[n] = f
        f = f * jnp.where(sub8 >= k, pltpu.roll(f, k, 0), 1.0)
    abuf[gi] = f[CH - 1 : CH, :]
    factor_copies = to_all(abuf.at[gi], as_, ar, line_peers)
    for i in range(ST):
        d = dp[steps(i), :]
        gp[steps(i), :] = jnp.sqrt(1.0 - d * d)
    ends[0] = jnp.where(sub8 >= 1, pltpu.roll(f, 1, 0), 1.0)
    ends[1] = total
    for load in load_spa:
        load.wait()
    multiply(xa, 0, ORDER, True)
    gather_pass(xa, gas, gar, copies)

    cross = []

    def line_factors():
        received(factor_copies)
        run = jnp.ones((1, RC), F32)
        places = [run] * 3
        for j in range(LINE):
            for n in range(3):
                places[n] = jnp.where(j == gi - n, run, places[n])
            if j >= LINE - 2:
                gabuf[gx, LINE - j] = run
            run = run * abuf[j]
        gabuf[gx, 0] = run
        gabuf[gx, 3] = abuf[LINE - 1]
        gabuf[gx, 4] = abuf[LINE - 2]
        cross.extend(to_all(gabuf.at[gx], a2s, a2r, cross_peers))
        for n in range(3):
            ends[2, n : n + 1, :] = places[n]
        run = jnp.ones((1, RC), F32)
        for j in range(3, LINE):
            run = run * jnp.where(j >= gi + 3, abuf[j - 2], 1.0)
        ends[3, 0:1, :] = run

    finish(xa, copies, line_factors)

    o = jnp.zeros((CH, RC), F32)
    for i in range(ST):
        o = dp[steps(i), :] * o + gp[steps(i), :] * mx[steps(i), :]
        mx[steps(i), :] = o
    for n, k in enumerate((1, 2, 4)):
        o = o + fstep[n] * jnp.where(sub8 >= k, pltpu.roll(o, k, 0), 0.0)
    bbuf[gi] = o[CH - 1 : CH, :]
    line_copies = to_all(bbuf.at[gi], bs, br, line_peers)

    received(table_copies)
    time_of = lax.broadcasted_iota(jnp.int32, (8, 128), 1)
    time_of = lax.rem(time_of, CH) * ST + time_of // CH
    for d in (1, 2):
        tabs[d] = jnp.where(tm + d < WINDOWS, tabs[d], DEAD)
    for d in range(3):
        local = lax.shift_right_arithmetic(tabs[d], 1) + (d - 2) * TW
        sel[8 * d : 8 * d + 8, :] = jnp.where(local == time_of, 1.0, 0.0)
    sel[24:32, :] = jnp.zeros((8, 128), F32)

    entry = jnp.where(sub8 >= 1, pltpu.roll(o, 1, 0), 0.0)
    for i in range(ST):
        mx[steps(i), :] = mx[steps(i), :] + fp[steps(i), :] * entry
    row_copies = hand_on(mx[...], chs, hs, hr)
    for i in range(ST):
        hx[steps(i), :] = fp[steps(i), :] * ends[0]
    factor_rows = hand_on(hx[...], ffs, fs, fr)
    received(cross)
    before = lax.rem(gx + LINES - 1, LINES)
    ends[3, 1:2, :] = jnp.where(gi >= 1, abuf[lax.rem(gi + LINE - 1, LINE)], gabuf[before, 3])
    ends[3, 2:3, :] = jnp.where(
        gi >= 2, abuf[lax.rem(gi + LINE - 2, LINE)], jnp.where(gi == 1, gabuf[before, 3], gabuf[before, 4])
    )
    received(line_copies)
    run = jnp.zeros((1, RC), F32)
    places = [run] * 3
    for j in range(LINE):
        for n in range(3):
            places[n] = jnp.where(j == gi - n, run, places[n])
        if j >= LINE - 2:
            tbuf[gx, LINE - j] = run
        run = abuf[j] * run + bbuf[j]
    tbuf[gx, 0] = run
    cross_copies = to_all(tbuf.at[gx], b2s, b2r, cross_peers)
    b = ends[1]
    for n, k in enumerate((1, 2, 4)):
        bstep[n] = b
        b = b * jnp.where(sub8 < CH - k, pltpu.roll(b, CH - k, 0), 1.0)
    ends[1] = jnp.where(sub8 < CH - 1, pltpu.roll(b, CH - 1, 0), 1.0)
    rest = jnp.ones((CH, RC), F32)
    for i in reversed(range(ST)):
        rp[steps(i), :] = rest
        rest = rest * dp[steps(i), :]
    received(factor_rows)
    received(row_copies)
    received(cross_copies)
    run = jnp.zeros((1, RC), F32)
    line_before = run
    for j in range(LINES):
        line_before = jnp.where(j == gx - 1, run, line_before)
        run = jnp.where(j < gx, gabuf[j, 0] * run + tbuf[j, 0], run)
    last, last_but = [tbuf[before, n] + gabuf[before, n] * line_before for n in (1, 2)]
    inside = [places[n] + ends[2, n : n + 1, :] * run for n in range(3)]
    entering = [
        inside[0],
        jnp.where(gi >= 1, inside[1], last),
        jnp.where(gi >= 2, inside[2], jnp.where(gi == 1, last, last_but)),
    ]
    own_second = second_block(0)
    picked = jnp.zeros((8, FB), F32)
    for d in range(3):
        state = jnp.where(own_second, entering[d][:, FB:], entering[d][:, :FB])
        picked = picked + (chs[d] + ffs[d] * state)
    load_tiles.wait()

    sub_fb = lax.broadcasted_iota(jnp.int32, (8, FB), 0)
    seen = jnp.zeros((8, 128), F32)
    for s in range(SLOTS):
        lhs = jnp.where(sub_fb == tblock[0, 0, s], picked[s : s + 1, :], 0.0).astype(BF16)
        seen = seen + lax.dot_general(lhs, tiles[s], NT, preferred_element_type=F32)
    obs[r] = seen
    received(to_all(obs.at[r], os_, or_, region_peers))
    observed = ((obs[0] + obs[1]) + obs[2]) + obs[3]
    weighted = (observed * noise[...]).astype(BF16).astype(F32)

    back = jnp.zeros((8, FB), F32)
    for s in range(SLOTS):
        row = jnp.sum(jnp.where(sub == tblock[0, 0, s], weighted, 0.0), axis=0, keepdims=True)
        lhs = jnp.where((sub == s) & live, row, 0.0).astype(BF16)
        back = back + jnp.dot(lhs, tiles[s], preferred_element_type=F32)
    bks[0] = back

    adds = []
    for d in range(3):
        term = ffs[d] * back
        adds.append(
            jnp.concatenate(
                [
                    jnp.sum(jnp.where(own_second, 0.0, term), axis=0, keepdims=True),
                    jnp.sum(jnp.where(own_second, term, 0.0), axis=0, keepdims=True),
                ],
                axis=1,
            )
        )
    one_down = adds[1] + ends[3, 1:2, :] * adds[0]
    cbuf[gi] = adds[2] + ends[3, 2:3, :] * one_down
    line_copies = to_all(cbuf.at[gi], cs, cr, line_peers)
    near[2] = adds[0]
    near[3] = one_down
    near_copies = [send(near.at[1 + d], near.at[d - 1], ns.at[d - 1], nr.at[d - 1], sooner[d - 1]) for d in (1, 2)]
    row_copies = [send(bks.at[0], bks.at[d], ks.at[d - 1], kr.at[d - 1], sooner[d - 1]) for d in (1, 2)]
    received(row_copies)
    rows = []
    for d in range(3):
        second = second_block(d)
        rows.append(
            jnp.concatenate([jnp.where(second, 0.0, bks[d]), jnp.where(second, bks[d], 0.0)], axis=1)
        )
    rows.append(jnp.zeros((8, RC), F32))
    first, second, third = thirds(jnp.concatenate(rows, axis=0))
    hot = sel[...].astype(BF16)
    hx[...] = (
        lax.dot_general(hot, third, TN, preferred_element_type=F32)
        + lax.dot_general(hot, second, TN, preferred_element_type=F32)
    ) + lax.dot_general(hot, first, TN, preferred_element_type=F32)

    c = jnp.zeros((CH, RC), F32)
    for i in reversed(range(ST)):
        h = hx[steps(i), :] + c
        hx[steps(i), :] = h
        c = dp[steps(i), :] * h
    for n, k in enumerate((1, 2, 4)):
        c = c + bstep[n] * jnp.where(sub8 < CH - k, pltpu.roll(c, CH - k, 0), 0.0)
    entry = jnp.where(sub8 < CH - 1, pltpu.roll(c, CH - 1, 0), 0.0)
    received(near_copies)
    close = jnp.where(tm + 1 < WINDOWS, near[0], 0.0) + jnp.where(tm + 2 < WINDOWS, near[1], 0.0)
    received(line_copies)
    run = jnp.zeros((1, RC), F32)
    for j in reversed(range(2, LINE)):
        run = abuf[j - 2] * run + cbuf[j]
    ubuf[gx, 0] = run
    ubuf[gx, 1] = cbuf[1]
    ubuf[gx, 2] = cbuf[0]
    cross_copies = to_all(ubuf.at[gx], c2s, c2r, cross_peers)
    mine = jnp.zeros((1, RC), F32)
    for j in reversed(range(3, LINE)):
        mine = jnp.where(j >= gi + 3, abuf[j - 2] * mine + cbuf[j], mine)
    received(cross_copies)
    zero = jnp.zeros((1, RC), F32)
    two, one, run = zero, zero, zero
    for j in reversed(range(1, LINES)):
        above = j > gx
        two = jnp.where(above, ubuf[j, 0] + gabuf[j, 2] * run, two)
        one = jnp.where(above, gabuf[j - 1, 3] * two + ubuf[j, 1], one)
        run = jnp.where(above, gabuf[j - 1, 4] * one + ubuf[j, 2], run)
    far = jnp.where(gi == LINE - 1, two, jnp.where(gi == LINE - 2, one, mine + ends[3, 0:1, :] * run))
    entry = entry + ends[1] * (close + far)

    def pulled_part(q):
        part = slice(KQ * q, KQ * (q + 1))
        for i in range(ST):
            held = hx[steps(i), part] + rp[steps(i), part] * entry[:, part]
            hx[steps(i), part] = gp[steps(i), part] * held
        xb[0, q] = lax.dot_general(
            moved, hx[:, part].astype(BF16), TN, preferred_element_type=F32
        ).astype(BF16)

    copies = gather_start(xb, gbs, gbr, pulled_part)
    multiply(xb, 0, ORDER, True)
    gather_pass(xb, gbs, gbr, copies)
    load_res.wait()
    res = resv[...]
    norm_here = whole(res * res)
    finish(xb, copies)

    image = dirv[...] + mx[...]
    imgv[...] = image
    store = pltpu.make_async_copy(imgv, img, lsem.at[12 + PIECES])
    store.start()

    def inverse(x):
        ok = x > 1e-37
        return jnp.where(ok, 1.0 / jnp.where(ok, x, 1.0), 0.0)

    res = resv[...]
    largest = jnp.max(jnp.max(jnp.abs(image), axis=0, keepdims=True), axis=1, keepdims=True)
    scaled = image * inverse(largest)
    stats = jnp.where(sub == 0, norm_here, 0.0)
    stats = jnp.where(sub == 1, whole(dirv[...] * image), stats)
    stats = jnp.where(sub == 2, whole(res * image), stats)
    stats = jnp.where(sub == 3, whole(scaled * scaled), stats)
    stats = jnp.where(sub == 4, largest, stats)

    def merged(buf, count):
        top = buf[0, 4:5, :]
        for j in range(1, count):
            top = jnp.maximum(top, buf[j, 4:5, :])
        inv = inverse(top)
        out = jnp.zeros((8, 128), F32)
        for j in range(count):
            scale = buf[j, 4:5, :] * inv
            out = out + jnp.where(sub == 3, buf[j] * (scale * scale), buf[j])
        return jnp.where(sub == 4, top, out)

    red1[gi] = stats
    older = list(sent)
    copies = to_all(red1.at[gi], r1s, r1r, line_peers)
    for c in older:
        c.wait_send()
    received(copies)
    here = gx * REGIONS + r
    store.wait()
    red2[here] = merged(red1, LINE)
    received(to_all(red2.at[here], r2s, r2r, plane_peers))
    stats = merged(red2, LINES * REGIONS)
    norm_old = stats[0:1, :]
    alpha = norm_old / stats[1:2, :]
    reach = alpha * stats[4:5, :]
    norm_new = jnp.maximum((norm_old - 2.0 * (alpha * stats[2:3, :])) + reach * (reach * stats[3:4, :]), 0.0)
    ab[...] = jnp.where(sub == 0, alpha, norm_new / norm_old)
    for c in sent[len(older) :]:
        c.wait_send()


def update(ab_h, img_h, dir_h, res_h, sol_h, sol_o, res_o, dir_o, ab, img, dirv, resv, sol, sn, rn, dn, asem, isem, osem):
    first = pltpu.make_async_copy(ab_h, ab, asem.at[0])
    first.start()
    loads = []
    for n in range(CUTS):
        rows = pl.ds(n * (TW // CUTS), TW // CUTS)
        loads.append(
            [
                pltpu.make_async_copy(far.at[rows], near.at[rows], isem.at[n, k])
                for k, (far, near) in enumerate(((img_h, img), (dir_h, dirv), (res_h, resv), (sol_h, sol)))
            ]
        )
        for load in loads[n]:
            load.start()
    first.wait()
    alpha, beta = ab[0:1, 0:1], ab[1:2, 0:1]
    stores = []
    for n in range(CUTS):
        rows = pl.ds(n * (TW // CUTS), TW // CUTS)
        for load in loads[n]:
            load.wait()
        left = resv[rows, :] - alpha * img[rows, :]
        rn[rows, :] = left
        sn[rows, :] = sol[rows, :] + alpha * dirv[rows, :]
        dn[rows, :] = left + beta * dirv[rows, :]
        for k, (near, far) in enumerate(((sn, sol_o), (rn, res_o), (dn, dir_o))):
            stores.append(pltpu.make_async_copy(near.at[rows], far.at[rows], osem.at[n, k]))
            stores[-1].start()
    for store in stores:
        store.wait()


def body(
    solution, residual, direction, decay, spatial, tiles,
    tile_block, tile_time, tile_cell, tile_count, noise_inv,
):
    hbm = pl.BlockSpec(memory_space=pltpu.HBM)
    vmem = pl.BlockSpec(memory_space=pltpu.VMEM)
    vector = (1, RC)
    dma = pltpu.SemaphoreType.DMA
    sems = [4, 13 + PIECES, 10, 10, 10, 10]
    for n in (LINE - 1, LINES - 1) * 3 + (2, 2, 2, 2, 2, REGIONS - 1, LINE - 1, LINES * REGIONS - 1):
        sems += [n, n]
    image, ab = pl.pallas_call(
        kernel,
        out_shape=(
            jax.ShapeDtypeStruct((TW, RC), F32),
            jax.ShapeDtypeStruct((8, 128), F32),
        ),
        in_specs=[hbm] * 10,
        out_specs=(hbm, vmem),
        scratch_shapes=[
            pltpu.SMEM((1, 1, SLOTS), jnp.int32),
            pltpu.SMEM((1, 1, SLOTS), jnp.int32),
            pltpu.SMEM((1, 1, SLOTS), jnp.int32),
            pltpu.VMEM((1, 1), jnp.int32),
            pltpu.VMEM((8, 128), F32),
            pltpu.VMEM((TW, RC), F32),
            pltpu.VMEM((TW, RC), F32),
            pltpu.VMEM((TW, RC), F32),
            pltpu.VMEM((PIECES, TW, 128), F32),
            pltpu.VMEM((REGIONS, RC, RC), BF16),
            pltpu.VMEM((SLOTS, 128, FB), BF16),
            pltpu.VMEM((REGIONS, RC // KQ, TW, KQ), BF16),
            pltpu.VMEM((REGIONS, RC // KQ, TW, KQ), BF16),
            pltpu.VMEM((TW, RC), F32),
            pltpu.VMEM((TW, RC), F32),
            pltpu.VMEM((TW, RC), F32),
            pltpu.VMEM((TW, RC), F32),
            pltpu.VMEM((TW, RC), F32),
            pltpu.VMEM((TW, RC), F32),
            pltpu.VMEM((3, CH, RC), F32),
            pltpu.VMEM((3, CH, RC), F32),
            pltpu.VMEM((4, CH, RC), F32),
            pltpu.VMEM((LINE,) + vector, F32),
            pltpu.VMEM((LINES, 5) + vector, F32),
            pltpu.VMEM((LINE,) + vector, F32),
            pltpu.VMEM((LINES, 3) + vector, F32),
            pltpu.VMEM((LINE,) + vector, F32),
            pltpu.VMEM((LINES, 3) + vector, F32),
            pltpu.VMEM((3, 8, 128), jnp.int32),
            pltpu.VMEM((5, 8, FB), F32),
            pltpu.VMEM((5, 8, FB), F32),
            pltpu.VMEM((3, 8, FB), F32),
            pltpu.VMEM((4,) + vector, F32),
            pltpu.VMEM((REGIONS, 8, 128), F32),
            pltpu.VMEM((LINE, 8, 128), F32),
            pltpu.VMEM((LINES * REGIONS, 8, 128), F32),
            pltpu.VMEM((32, 128), F32),
        ]
        + [dma((n,)) for n in sems],
        compiler_params=pltpu.CompilerParams(
            collective_id=0, has_side_effects=True, vmem_limit_bytes=62 << 20
        ),
        cost_estimate=pl.CostEstimate(
            flops=4 * TW * RC * RC * REGIONS, bytes_accessed=12 << 20, transcendentals=TW * RC
        ),
        name="cg_step",
    )(direction, residual, decay, spatial, tiles, tile_block, tile_time, tile_cell, tile_count, noise_inv)
    block = jax.ShapeDtypeStruct((TW, RC), F32)
    return pl.pallas_call(
        update,
        out_shape=(block,) * 3,
        in_specs=[hbm] * 5,
        out_specs=(hbm,) * 3,
        scratch_shapes=[pltpu.VMEM((8, 128), F32)]
        + [pltpu.VMEM((TW, RC), F32)] * 7
        + [dma((1,)), dma((CUTS, 4)), dma((CUTS, 3))],
        cost_estimate=pl.CostEstimate(flops=6 * TW * RC, bytes_accessed=28 * TW * RC, transcendentals=0),
        name="cg_update",
    )(ab, image, direction, residual, solution)


def solution(mesh):
    return jax.shard_map(
        body,
        mesh=mesh,
        in_specs=(
            P("tm", "region"),
            P("tm", "region"),
            P("tm", "region"),
            P("tm", "region"),
            P("region", None),
            P("tm", "region", None, None, None),
            P("tm", "region", None),
            P("tm", "region", None),
            P("tm", "region", None),
            P("tm", "region"),
            P("tm", None),
        ),
        out_specs=(P("tm", "region"), P("tm", "region"), P("tm", "region")),
        check_vma=False,
    )
```
